32 devices in a mesh: dp: 4 (over z), seq: 8 (over y, x, core).
Axes of the slice: x: 2, y: 2, z: 4, core: 2. Of those that a mesh axis runs over, the one named last changes fastest.
Arguments:
- queries: bfloat16 [4096, 4096], P(('dp', 'seq')), may hold values from -6 to 6
- keys: bfloat16 [4096, 512], P(('dp', 'seq')), may hold values from -6 to 6
- values: bfloat16 [4096, 512], P(('dp', 'seq')), may hold values from -6 to 6
- grad_out: bfloat16 [4096, 4096], P(('dp', 'seq')), may hold values from -6 to 6
- doc_lengths: int32 [16], replicated, may hold values from 1 to 1024, 4096 in all
Outputs:
- grad_q: bfloat16 [4096, 4096], P(('dp', 'seq'))
- grad_k: bfloat16 [4096, 512], P(('dp', 'seq'))
- grad_v: bfloat16 [4096, 512], P(('dp', 'seq'))
The draws below stay inside these ranges and needn't reach their ends.
Inputs may be any that keep to these rules, and one draw needn't show every extreme that they name: `doc_lengths`: the 16 lengths sum to 4096; the longest is exactly 1024.
All inputs are finite; a program needn't handle non-finite values.
Results may differ from the reference program's by a relative error of at most 0.0071.
Values may be sent and summed in bfloat16 or wider, within the bound.
No kernel may reach another device: no remote copies, remote signals or barrier semaphores. Data moves between devices by JAX's collectives and lax.ppermute only.
A program may use at most 64 MiB of HBM per device.

```python
import math
import jax
import jax.numpy as jnp
import numpy as np
from jax import lax

QH = 32
KVH = 4
HD = 128
TOK_DEV = 128
GROUP_TOK = 1024
TOKENS = 4096
DOCS = 16
N_DP = 4
N_SEQ = 8


def draw_queries(key, part):
    own_key = jax.random.fold_in(key, 11)
    result = jnp.clip(jax.random.normal(own_key, (TOKENS, QH * HD), jnp.float32), -6.0, 6.0)
    return result.astype(jnp.bfloat16)


def draw_keys(key, part):
    own_key = jax.random.fold_in(key, 12)
    result = jnp.clip(jax.random.normal(own_key, (TOKENS, KVH * HD), jnp.float32), -6.0, 6.0)
    return result.astype(jnp.bfloat16)


def levels(key, extent, cuts, low, largest):
    loudness = 1.0
    for position, parts in cuts:
        steps = jax.random.uniform(jax.random.fold_in(jax.random.fold_in(key, 6), position), (parts,), jnp.float32, low / len(cuts), largest / len(cuts))
        loudness = loudness * jnp.repeat(jnp.exp(steps), extent[position] // parts).reshape((-1,) + (1,) * (len(extent) - 1 - position))
    return loudness


def split_up(count, total, bound, skew):
    portions = [(1 << 20) // math.isqrt(standing ** skew) + 1 for standing in range(2, count + 1)]
    rest, holding = total - bound - (count - 1), [1] * (count - 1)
    while rest > 0:
        movable = [i for i in range(count - 1) if holding[i] < bound]
        pool, budget = sum([portions[i] for i in movable]), rest
        for i in movable:
            more = min(bound - holding[i], max(1, budget * portions[i] // pool), rest)
            holding[i] = holding[i] + more
            rest = rest - more
    return np.array([bound] + holding)


def uneven_parts(rng, count, total, limit, lean):
    if count == 2:
        one = jax.random.randint(rng, (), max(1, total - limit), min(limit, total - 1) + 1)
        return jnp.stack([one, total - one])
    tallies = jnp.asarray(split_up(count, total, limit, lean), jnp.int32)
    twos = (count - 1) // 2
    source_of, receiver = tallies[1:1 + 2 * twos:2], tallies[2:2 + 2 * twos:2]
    slack = jnp.minimum(source_of - 1, limit - receiver)
    shifted = jax.random.randint(jax.random.fold_in(rng, 1), (twos,), 0, 1 << 20) % (slack + 1)
    tallies = tallies.at[1:1 + 2 * twos:2].set(source_of - shifted).at[2:2 + 2 * twos:2].set(receiver + shifted)
    return tallies[jax.random.permutation(jax.random.fold_in(rng, 2), count)]


def normal_values(stream_key, shape, width, bound, shards=(), held_as=jnp.bfloat16):
    values = jax.random.normal(stream_key, shape, jnp.float32) * width
    if len(shards) > 0:
        values = levels(stream_key, shape, shards, -0.22, 0.18) * values
    return jnp.clip(values, min=-bound, max=bound).astype(held_as)


def setup_inputs(seed: int = 0) -> dict:
    seeds = jax.random.split(jax.random.key(seed), 6)
    queries = draw_queries(jax.random.fold_in(seeds[5], 71), 0)
    keys = draw_keys(jax.random.fold_in(seeds[5], 71), 0)
    values = normal_values(seeds[2], (TOKENS, KVH * HD), 1.0, 6.0, ((0, 32),))
    grad_out = normal_values(seeds[3], (TOKENS, QH * HD), 1.0, 6.0, ((0, 32),))
    doc_lengths = uneven_parts(seeds[4], DOCS, TOKENS, GROUP_TOK, 2).astype(jnp.int32)
    return dict(queries=queries, keys=keys, values=values, grad_out=grad_out, doc_lengths=doc_lengths)


def doc_index(positions, doc_ends):
    inside = (positions[:, None] >= doc_ends[None, :]).astype(jnp.int32)
    return jnp.sum(inside, axis=1).astype(jnp.int32) - (positions < 0).astype(jnp.int32)


def reference(queries, keys, values, grad_out, doc_lengths):
    group_len = TOK_DEV * N_SEQ
    per_kv = QH // KVH
    inv_root = HD ** -0.5
    doc_ends = jnp.cumsum(doc_lengths).astype(jnp.int32)
    q_groups = queries.reshape(N_DP, group_len, QH, HD)
    o_groups = grad_out.reshape(N_DP, group_len, QH, HD)
    zero_rows = jnp.zeros((group_len, KVH * HD), jnp.bfloat16)
    k_padded = jnp.concatenate([zero_rows, keys], 0).reshape(N_DP + 1, group_len, KVH, HD)
    v_padded = jnp.concatenate([zero_rows, values], 0).reshape(N_DP + 1, group_len, KVH, HD)
    zero_index = jnp.zeros((), jnp.int32)

    def one_group(state_now, inputs):
        acc_k, acc_v = state_now
        grp_index, q_grp, o_grp = inputs
        grp_index = grp_index.astype(jnp.int32)
        k_window = lax.dynamic_slice_in_dim(k_padded, grp_index, 2, 0).reshape(2 * group_len, KVH, HD)
        v_window = lax.dynamic_slice_in_dim(v_padded, grp_index, 2, 0).reshape(2 * group_len, KVH, HD)
        q_pos = grp_index * group_len + jnp.arange(group_len, dtype=jnp.int32)
        k_pos = (grp_index - 1) * group_len + jnp.arange(2 * group_len, dtype=jnp.int32)
        allowed = (doc_index(q_pos, doc_ends)[:, None] == doc_index(k_pos, doc_ends)[None, :]) & (k_pos[None, :] <= q_pos[:, None])

        def per_head(pieces):
            q_head, o_head, head_idx = pieces
            kv_idx = (head_idx // per_kv).astype(jnp.int32)
            k_head = lax.dynamic_index_in_dim(k_window, kv_idx, 1, keepdims=False)
            v_head = lax.dynamic_index_in_dim(v_window, kv_idx, 1, keepdims=False)
            scores = jnp.dot(q_head, k_head.T, preferred_element_type=jnp.float32) * inv_root
            scores = jnp.where(allowed, scores, -1e30)
            row_peak = jnp.max(scores, axis=1, keepdims=True)
            log_norm = row_peak + jnp.log(jnp.sum(jnp.where(allowed, jnp.exp(scores - row_peak), 0.0), axis=1, keepdims=True))
            prob_f = jnp.where(allowed, jnp.exp(scores - log_norm), 0.0)
            dprobs = jnp.dot(o_head, v_head.T, preferred_element_type=jnp.float32)
            row_delta = jnp.sum(prob_f * dprobs, axis=1, keepdims=True)
            probs_b = prob_f.astype(jnp.bfloat16)
            dscores = (prob_f * (dprobs - row_delta)).astype(jnp.bfloat16)
            grad_qh = (jnp.dot(dscores, k_head, preferred_element_type=jnp.float32) * inv_root).astype(jnp.bfloat16)
            grad_kh = jnp.dot(dscores.T, q_head, preferred_element_type=jnp.float32) * inv_root
            grad_vh = jnp.dot(probs_b.T, o_head, preferred_element_type=jnp.float32)
            return grad_qh, grad_kh, grad_vh

        head_ids = jnp.arange(QH, dtype=jnp.int32)
        grad_qs, grad_ks, grad_vs = lax.map(per_head, (q_grp.transpose(1, 0, 2), o_grp.transpose(1, 0, 2), head_ids))
        grad_ks = grad_ks.reshape(KVH, per_kv, 2 * group_len, HD).sum(1).transpose(1, 0, 2).reshape(2, group_len, KVH, HD)
        grad_vs = grad_vs.reshape(KVH, per_kv, 2 * group_len, HD).sum(1).transpose(1, 0, 2).reshape(2, group_len, KVH, HD)
        begin_at = (grp_index, zero_index, zero_index, zero_index)
        acc_k = lax.dynamic_update_slice(acc_k, lax.dynamic_slice(acc_k, begin_at, (2, group_len, KVH, HD)) + grad_ks, begin_at)
        acc_v = lax.dynamic_update_slice(acc_v, lax.dynamic_slice(acc_v, begin_at, (2, group_len, KVH, HD)) + grad_vs, begin_at)
        return (acc_k, acc_v), grad_qs.transpose(1, 0, 2)

    start_acc = jnp.zeros((N_DP + 1, group_len, KVH, HD), jnp.float32)
    group_ids = jnp.arange(N_DP, dtype=jnp.int32)
    (acc_k, acc_v), grad_q = lax.scan(one_group, (start_acc, start_acc), (group_ids, q_groups, o_groups))
    grad_q = grad_q.reshape(TOKENS, QH * HD)
    grad_k = acc_k[1:].reshape(TOKENS, KVH * HD).astype(jnp.bfloat16)
    grad_v = acc_v[1:].reshape(TOKENS, KVH * HD).astype(jnp.bfloat16)
    return grad_q, grad_k, grad_v
```

```python
import functools

import jax
import jax.numpy as jnp
from jax import lax
from jax.experimental import pallas as pl
from jax.experimental.pallas import tpu as pltpu
from jax.sharding import PartitionSpec as P

QH = 32
KVH = 4
HD = 128
LOG2E = 1.4426950408889634
NT = (((1,), (1,)), ((), ()))
NN = (((1,), (0,)), ((), ()))
TN = (((0,), (0,)), ((), ()))


def dot(a, b, dims):
    return lax.dot_general(a, b, dims, preferred_element_type=jnp.float32)


def attend_kernel(
    dp_count,
    seq_count,
    info_ref,
    doc_ref,
    q_mine,
    q_theirs,
    o_mine,
    o_theirs,
    *refs,
):
    pairs = seq_count // 2
    kv_refs = refs[: pairs + 1]
    dq_mine, dq_theirs, own_out = refs[pairs + 1 : pairs + 4]
    part_outs = refs[pairs + 4 : 2 * pairs + 4]
    kv_all, prob_s, dprob_s, peak_s, pb_s, ds_s, dq_s, dkv_s = refs[2 * pairs + 4 :]
    tok = q_mine.shape[1]
    per_kv = QH // KVH
    lanes = per_kv * tok
    chunk = 2 * tok
    inv_root = HD ** -0.5
    dp_idx = info_ref[0]
    seq_idx = info_ref[1]
    core = lax.rem(seq_idx, 2)
    pair = seq_idx // 2
    docs = doc_ref.shape[0]

    kv_all[0] = kv_refs[0][...]
    kv_all[pairs] = kv_refs[pairs][...]
    for k in range(1, pairs):
        dist = lax.rem(pair - (pair ^ k) + pairs, pairs)
        kv_all[dist] = kv_refs[k][...]
    dkv_s[...] = jnp.zeros_like(dkv_s)

    key_iota = lax.broadcasted_iota(jnp.int32, (tok, tok), 0)
    tok_iota = lax.broadcasted_iota(jnp.int32, (tok, tok), 1)

    for half in range(2):
        q_ref, o_ref, dq_ref = ((q_mine, o_mine, dq_mine), (q_theirs, o_theirs, dq_theirs))[half]
        here = dp_idx * seq_count + (seq_idx ^ half)
        first = here * tok
        pos = first + tok_iota
        starts = jnp.zeros_like(pos)
        low = first * 0
        end = first * 0
        for d in range(docs):
            end = end + doc_ref[d]
            starts = jnp.where(pos >= end, end, starts)
            low = jnp.where(first >= end, end, low)
        count = here - low // tok + 1

        for g in range(2):
            heads = pl.ds(g * per_kv, per_kv)
            q_stack = q_ref.at[heads].reshape(lanes, HD)
            o_stack = o_ref.at[heads].reshape(lanes, HD)

            def tile_of(back):
                tile = here - back
                dist = here // 2 - tile // 2
                row = pl.multiple_of((lax.rem(tile, 2) ^ core) * tok, tok)
                return tile, dist, row

            def stat_step(back, state):
                tile, dist, row = tile_of(back)
                k_tile = kv_all[dist, pl.ds(row, tok), pl.ds(g * HD, HD)]
                v_tile = kv_all[dist, pl.ds(row, tok), pl.ds((2 + g) * HD, HD)]
                key_pos = tile * tok + key_iota
                bias = jnp.where((key_pos >= starts) & (key_pos <= pos), 0.0, -1e30)
                bias = jnp.concatenate([bias, bias], 1)
                out = []
                for c in range(lanes // chunk):
                    peak, total, mixed = state[c]
                    cols = pl.ds(c * chunk, chunk)
                    scores = dot(k_tile, q_stack[cols, :], NT) * (inv_root * LOG2E) + bias
                    dprobs = dot(v_tile, o_stack[cols, :], NT)
                    new_peak = jnp.maximum(peak, jnp.max(scores, 0, keepdims=True))
                    weights = jnp.exp2(scores - new_peak)
                    rescale = jnp.exp2(peak - new_peak)
                    total = total * rescale + jnp.sum(weights, 0, keepdims=True)
                    mixed = mixed * rescale + jnp.sum(weights * dprobs, 0, keepdims=True)
                    prob_s[back, :, cols] = weights
                    dprob_s[back, :, cols] = dprobs
                    peak_s[back, :, cols] = new_peak
                    out.append((new_peak, total, mixed))
                return tuple(out)

            zero = jnp.zeros((1, chunk), jnp.float32)
            start = tuple((zero - 1e30, zero, zero) for _ in range(lanes // chunk))
            state = lax.fori_loop(0, count, stat_step, start)
            dq_s[...] = jnp.zeros_like(dq_s)
            final = [
                (peak, 1.0 / total, mixed / total) for peak, total, mixed in state
            ]

            def grad_step(back, carry):
                tile, dist, row = tile_of(back)
                rows = pl.ds(row, tok)
                k_tile = kv_all[dist, rows, pl.ds(g * HD, HD)]
                for c in range(lanes // chunk):
                    peak, inv_total, delta = final[c]
                    cols = pl.ds(c * chunk, chunk)
                    factor = jnp.exp2(peak_s[back, :, cols] - peak) * inv_total
                    probs = prob_s[back, :, cols] * factor
                    pb_s[:, cols] = probs.astype(jnp.bfloat16)
                    ds_s[:, cols] = (probs * (dprob_s[back, :, cols] - delta)).astype(jnp.bfloat16)
                dk_cols = pl.ds(g * HD, HD)
                dv_cols = pl.ds((2 + g) * HD, HD)
                dkv_s[dist, rows, dv_cols] += dot(pb_s[...], o_stack[...], NN)
                dkv_s[dist, rows, dk_cols] += dot(ds_s[...], q_stack[...], NN) * inv_root
                dq_s[...] += dot(k_tile, ds_s[...], TN)
                return carry

            lax.fori_loop(0, count, grad_step, 0)
            for h in range(per_kv):
                block = dq_s[:, pl.ds(h * tok, tok)] * inv_root
                dq_ref[:, pl.ds((g * per_kv + h) * HD, HD)] = block.T.astype(jnp.bfloat16)

    own_out[...] = dkv_s[0]
    part_outs[pairs - 1][...] = dkv_s[pairs].astype(jnp.bfloat16)
    for k in range(1, pairs):
        dist = lax.rem(pair - (pair ^ k) + pairs, pairs)
        part_outs[k - 1][...] = dkv_s[dist].astype(jnp.bfloat16)


def attend(info, doc_lengths, q_mine, q_theirs, o_mine, o_theirs, blocks, dp_count, seq_count):
    tok = q_mine.shape[1]
    pairs = seq_count // 2
    tiles = seq_count + 1
    lanes = (QH // KVH) * tok
    rows, cols = blocks[0].shape
    dq_shape = jax.ShapeDtypeStruct((tok, QH // 2 * HD), jnp.bfloat16)
    part = jax.ShapeDtypeStruct((rows, cols), jnp.bfloat16)
    out_shape = [dq_shape, dq_shape, jax.ShapeDtypeStruct((rows, cols), jnp.float32)] + [part] * pairs
    vmem = pl.BlockSpec(memory_space=pltpu.VMEM)
    smem = pl.BlockSpec(memory_space=pltpu.SMEM)
    return pl.pallas_call(
        functools.partial(attend_kernel, dp_count, seq_count),
        out_shape=out_shape,
        in_specs=[smem, smem] + [vmem] * (4 + len(blocks)),
        out_specs=[vmem] * len(out_shape),
        scratch_shapes=[
            pltpu.VMEM((pairs + 1, rows, cols), jnp.bfloat16),
            pltpu.VMEM((tiles, tok, lanes), jnp.float32),
            pltpu.VMEM((tiles, tok, lanes), jnp.float32),
            pltpu.VMEM((tiles, 1, lanes), jnp.float32),
            pltpu.VMEM((tok, lanes), jnp.bfloat16),
            pltpu.VMEM((tok, lanes), jnp.bfloat16),
            pltpu.VMEM((HD, lanes), jnp.float32),
            pltpu.VMEM((pairs + 1, rows, cols), jnp.float32),
        ],
        compiler_params=pltpu.CompilerParams(vmem_limit_bytes=48 * 1024 * 1024),
        name="attend",
    )(info, doc_lengths, q_mine, q_theirs, o_mine, o_theirs, *blocks)


def local(queries, keys, values, grad_out, doc_lengths):
    tok = queries.shape[0]
    dp_count = lax.axis_size("dp")
    seq_count = lax.axis_size("seq")
    pairs = seq_count // 2
    dp_idx = lax.axis_index("dp")
    seq_idx = lax.axis_index("seq")
    core = lax.rem(seq_idx, 2)
    pair = seq_idx // 2
    half_kv = KVH // 2 * HD

    def swap(value, k):
        return lax.ppermute(value, "seq", [(i, i ^ k) for i in range(seq_count)])

    def kv_half(which):
        return jnp.concatenate(
            [lax.dynamic_slice_in_dim(t, which * half_kv, half_kv, 1) for t in (keys, values)], 1
        )

    own = jnp.concatenate([kv_half(core), swap(kv_half(1 - core), 1)], 0)
    prev = lax.ppermute(own, "dp", [(i, i + 1) for i in range(dp_count - 1)])

    def head_half(tensor, which):
        heads = tensor.reshape(tok, 2, QH // 2, HD)
        return lax.dynamic_index_in_dim(heads, which, 1, keepdims=False).transpose(1, 0, 2)

    q_theirs = swap(head_half(queries, 1 - core), 1)
    o_theirs = swap(head_half(grad_out, 1 - core), 1)
    q_mine = head_half(queries, core)
    o_mine = head_half(grad_out, core)

    blocks = [own]
    for k in range(1, pairs):
        blocks.append(swap(jnp.where((pair ^ k) > pair, own, prev), 2 * k))
    blocks.append(prev)
    info = jnp.stack([dp_idx, seq_idx]).astype(jnp.int32)
    outs = attend(info, doc_lengths, q_mine, q_theirs, o_mine, o_theirs, blocks, dp_count, seq_count)
    dq_mine, dq_theirs, own_sum = outs[:3]
    dq_other = swap(dq_theirs, 1)
    prev_sum = outs[-1].astype(jnp.float32)
    for k in range(1, pairs):
        back = swap(outs[2 + k], 2 * k).astype(jnp.float32)
        later = (pair ^ k) > pair
        own_sum = own_sum + jnp.where(later, back, 0.0)
        prev_sum = prev_sum + jnp.where(later, 0.0, back)
    from_next = lax.ppermute(
        prev_sum.astype(jnp.bfloat16), "dp", [(i + 1, i) for i in range(dp_count - 1)]
    )
    total = (own_sum + from_next.astype(jnp.float32)).astype(jnp.bfloat16)
    mine, other = total[:tok], swap(total[tok:], 1)

    def join(a, b):
        low = jnp.where(core == 0, a, b)
        high = jnp.where(core == 0, b, a)
        return jnp.concatenate([low, high], 1)

    grad_q = join(dq_mine, dq_other)
    grad_k = join(mine[:, :half_kv], other[:, :half_kv])
    grad_v = join(mine[:, half_kv:], other[:, half_kv:])
    return (grad_q, grad_k, grad_v)


def solution(mesh):
    spec = P(("dp", "seq"), None)
    return jax.shard_map(
        local,
        mesh=mesh,
        in_specs=(spec, spec, spec, spec, P()),
        out_specs=(spec, spec, spec),
        check_vma=False,
    )
```

```python
import functools

import jax
import jax.numpy as jnp
from jax import lax
from jax.experimental import pallas as pl
from jax.experimental.pallas import tpu as pltpu
from jax.sharding import PartitionSpec as P

QH = 32
KVH = 4
HD = 128
PER_KV = QH // KVH
LOG2E = 1.4426950408889634
NT = (((1,), (1,)), ((), ()))
NN = (((1,), (0,)), ((), ()))
TN = (((0,), (0,)), ((), ()))


def dot(a, b, dims):
    return lax.dot_general(a, b, dims, preferred_element_type=jnp.float32)


def distance(pair, k, pairs):
    return lax.rem(pair - (pair ^ k) + pairs, pairs)


def attend_kernel(seq_count, info_ref, doc_ref, q_mine, o_mine, qo_theirs, *refs):
    pairs = seq_count // 2
    kv_refs = refs[: pairs + 1]
    dq_mine, dq_theirs, own_out = refs[pairs + 1 : pairs + 4]
    part_outs = refs[pairs + 4 : 2 * pairs + 4]
    kv_all, prob_s, dprob_s, peak_s, stat_s, dq_s, dkv_s = refs[2 * pairs + 4 :]
    tok = q_mine.shape[0]
    keys = 2 * tok
    lanes = PER_KV * tok
    inv_root = HD ** -0.5
    seq_idx = info_ref[1]
    core = lax.rem(seq_idx, 2)
    pair = seq_idx // 2
    chip = info_ref[0] * pairs + pair

    kv_all[0] = kv_refs[0][...]
    kv_all[pairs] = kv_refs[pairs][...]
    for k in range(1, pairs):
        kv_all[distance(pair, k, pairs)] = kv_refs[k][...]
    dkv_s[...] = jnp.zeros_like(dkv_s)
    dq_s[...] = jnp.zeros_like(dq_s)
    stat_s[0] = jnp.full_like(stat_s[0], -1e30)
    stat_s[1] = jnp.zeros_like(stat_s[1])
    stat_s[2] = jnp.zeros_like(stat_s[2])

    row = lax.broadcasted_iota(jnp.int32, (keys, tok), 0)
    row = ((row // tok) ^ core) * tok + lax.rem(row, tok)
    first = chip * keys
    pos = [
        first + (core ^ half) * tok + lax.broadcasted_iota(jnp.int32, (1, tok), 1)
        for half in range(2)
    ]
    starts = [jnp.zeros_like(p) for p in pos]
    low = first * 0
    end = first * 0
    for d in range(doc_ref.shape[0]):
        end = end + doc_ref[d]
        low = jnp.where(first >= end, end, low)
        starts = [jnp.where(p >= end, end, s) for p, s in zip(pos, starts)]
    count = chip - low // keys + 1

    def pieces():
        for half in range(2):
            for c in range(PER_KV // 2):
                yield half, c, pl.ds(half * lanes + c * keys, keys)

    def rows_of(ref, c):
        return jnp.concatenate(
            [ref[:, pl.ds((2 * c + i) * HD, HD)] for i in range(2)], 0
        )

    def q_rows(half, c):
        return rows_of((q_mine, qo_theirs.at[0])[half], c)

    def o_rows(half, c):
        return rows_of((o_mine, qo_theirs.at[1])[half], c)

    def stat_step(back, carry):
        k_tile = kv_all[back, :, pl.ds(0, HD)]
        v_tile = kv_all[back, :, pl.ds(HD, HD)]
        key_pos = (chip - back) * keys + row
        biases = []
        for half in range(2):
            bias = jnp.where((key_pos >= starts[half]) & (key_pos <= pos[half]), 0.0, -1e30)
            biases.append(jnp.concatenate([bias, bias], 1))
        for half, c, cols in pieces():
            peak = stat_s[0, :, cols]
            scores = dot(k_tile, q_rows(half, c), NT) * (inv_root * LOG2E) + biases[half]
            dprobs = dot(v_tile, o_rows(half, c), NT)
            new_peak = jnp.maximum(peak, jnp.max(scores, 0, keepdims=True))
            weights = jnp.exp2(scores - new_peak)
            rescale = jnp.exp2(peak - new_peak)
            stat_s[0, :, cols] = new_peak
            stat_s[1, :, cols] = stat_s[1, :, cols] * rescale + jnp.sum(weights, 0, keepdims=True)
            stat_s[2, :, cols] = stat_s[2, :, cols] * rescale + jnp.sum(
                weights * dprobs, 0, keepdims=True
            )
            prob_s[back, :, cols] = weights
            dprob_s[back, :, cols] = dprobs
            peak_s[back, :, cols] = new_peak
        return carry

    lax.fori_loop(0, count, stat_step, 0)
    inv_total = 1.0 / stat_s[1]
    stat_s[1] = inv_total
    stat_s[2] = stat_s[2] * inv_total

    def grad_step(back, carry):
        k_tile = kv_all[back, :, pl.ds(0, HD)]
        dk = jnp.zeros((keys, HD), jnp.float32)
        dv = jnp.zeros((keys, HD), jnp.float32)
        for half, c, cols in pieces():
            factor = jnp.exp2(peak_s[back, :, cols] - stat_s[0, :, cols]) * stat_s[1, :, cols]
            probs = prob_s[back, :, cols] * factor
            probs_b = probs.astype(jnp.bfloat16)
            dscores = (probs * (dprob_s[back, :, cols] - stat_s[2, :, cols])).astype(jnp.bfloat16)
            dv = dv + dot(probs_b, o_rows(half, c), NN)
            dk = dk + dot(dscores, q_rows(half, c), NN)
            dq_s[:, cols] += dot(k_tile, dscores, TN)
        dkv_s[back, :, pl.ds(0, HD)] = dk * inv_root
        dkv_s[back, :, pl.ds(HD, HD)] = dv
        return carry

    lax.fori_loop(0, count, grad_step, 0)
    own_out[...] = dkv_s[0]
    part_outs[pairs - 1][...] = dkv_s[pairs].astype(jnp.bfloat16)
    for k in range(1, pairs):
        part_outs[k - 1][...] = dkv_s[distance(pair, k, pairs)].astype(jnp.bfloat16)
    for half, dq_ref in enumerate((dq_mine, dq_theirs)):
        for h in range(PER_KV):
            block = dq_s[:, pl.ds(half * lanes + h * tok, tok)] * inv_root
            dq_ref[:, pl.ds(h * HD, HD)] = block.T.astype(jnp.bfloat16)


def attend(g, info, doc_lengths, queries, grad_out, qo_theirs, blocks, seq_count):
    tok = queries.shape[0]
    pairs = seq_count // 2
    lanes = PER_KV * tok
    keys, cols = blocks[0].shape
    width = PER_KV * HD
    dq_shape = jax.ShapeDtypeStruct((tok, width), jnp.bfloat16)
    part = jax.ShapeDtypeStruct((keys, cols), jnp.bfloat16)
    out_shape = [dq_shape, dq_shape, jax.ShapeDtypeStruct((keys, cols), jnp.float32)] + [part] * pairs
    smem = pl.BlockSpec(memory_space=pltpu.SMEM)
    mine = pl.BlockSpec((tok, width), lambda i, info: (0, 2 * lax.rem(info[1], 2) + g))
    whole = pl.BlockSpec((keys, cols), lambda i, info: (0, 0))
    dq_spec = pl.BlockSpec((tok, width), lambda i, info: (0, 0))
    grid_spec = pltpu.PrefetchScalarGridSpec(
        num_scalar_prefetch=1,
        grid=(1,),
        in_specs=[
            smem,
            mine,
            mine,
            pl.BlockSpec((2, tok, width), lambda i, info: (0, 0, g)),
        ]
        + [whole] * len(blocks),
        out_specs=[dq_spec, dq_spec] + [whole] * (pairs + 1),
        scratch_shapes=[
            pltpu.VMEM((pairs + 1, keys, cols), jnp.bfloat16),
            pltpu.VMEM((pairs + 1, keys, 2 * lanes), jnp.float32),
            pltpu.VMEM((pairs + 1, keys, 2 * lanes), jnp.float32),
            pltpu.VMEM((pairs + 1, 1, 2 * lanes), jnp.float32),
            pltpu.VMEM((3, 1, 2 * lanes), jnp.float32),
            pltpu.VMEM((HD, 2 * lanes), jnp.float32),
            pltpu.VMEM((pairs + 1, keys, cols), jnp.float32),
        ],
    )
    return pl.pallas_call(
        functools.partial(attend_kernel, seq_count),
        out_shape=out_shape,
        grid_spec=grid_spec,
        compiler_params=pltpu.CompilerParams(vmem_limit_bytes=56 * 1024 * 1024),
        cost_estimate=pl.CostEstimate(
            flops=10 * keys * 2 * lanes * HD * (pairs + 1),
            bytes_accessed=8 * 1024 * 1024,
            transcendentals=keys * 2 * lanes * (pairs + 1),
        ),
        name="attend_%d" % g,
    )(info, doc_lengths, queries, grad_out, qo_theirs, *blocks)


def local(queries, keys, values, grad_out, doc_lengths):
    tok = queries.shape[0]
    dp_count = lax.axis_size("dp")
    seq_count = lax.axis_size("seq")
    pairs = seq_count // 2
    dp_idx = lax.axis_index("dp")
    seq_idx = lax.axis_index("seq")
    core = lax.rem(seq_idx, 2)
    pair = seq_idx // 2
    groups = KVH // 2

    def swap(value, k):
        return lax.ppermute(value, "seq", [(i, i ^ k) for i in range(seq_count)])

    def kv_half(which):
        return [
            jnp.concatenate(
                [
                    lax.dynamic_slice_in_dim(t, (which * groups + g) * HD, HD, 1)
                    for t in (keys, values)
                ],
                1,
            )
            for g in range(groups)
        ]

    received = swap(jnp.stack(kv_half(1 - core)), 1)
    own = [jnp.concatenate([m, received[g]], 0) for g, m in enumerate(kv_half(core))]
    prev = [
        lax.ppermute(o, "dp", [(i, i + 1) for i in range(dp_count - 1)]) for o in own
    ]
    width = QH // 2 * HD
    qo_theirs = swap(
        jnp.stack(
            [lax.dynamic_slice_in_dim(t, (1 - core) * width, width, 1) for t in (queries, grad_out)]
        ),
        1,
    )
    info = jnp.stack([dp_idx, seq_idx]).astype(jnp.int32)

    blocks = []
    for g in range(groups):
        sent = [swap(jnp.where((pair ^ k) > pair, own[g], prev[g]), 2 * k) for k in range(1, pairs)]
        blocks.append([own[g]] + sent + [prev[g]])
    dq_mine, dq_other, totals = [], [], []
    for g in range(groups):
        outs = attend(g, info, doc_lengths, queries, grad_out, qo_theirs, blocks[g], seq_count)
        dq_mine.append(outs[0])
        dq_other.append(swap(outs[1], 1))
        own_sum = outs[2]
        prev_sum = outs[-1].astype(jnp.float32)
        for k in range(1, pairs):
            back = swap(outs[2 + k], 2 * k).astype(jnp.float32)
            later = (pair ^ k) > pair
            own_sum = own_sum + jnp.where(later, back, 0.0)
            prev_sum = prev_sum + jnp.where(later, 0.0, back)
        from_next = lax.ppermute(
            prev_sum.astype(jnp.bfloat16), "dp", [(i + 1, i) for i in range(dp_count - 1)]
        )
        totals.append((own_sum + from_next.astype(jnp.float32)).astype(jnp.bfloat16))
    mine = [t[:tok] for t in totals]
    other = [swap(t[tok:], 1) for t in totals]

    def join(a, b):
        low = [jnp.where(core == 0, x, y) for x, y in zip(a, b)]
        high = [jnp.where(core == 0, y, x) for x, y in zip(a, b)]
        return jnp.concatenate(low + high, 1)

    grad_q = join(dq_mine, dq_other)
    grad_k = join([m[:, :HD] for m in mine], [o[:, :HD] for o in other])
    grad_v = join([m[:, HD:] for m in mine], [o[:, HD:] for o in other])
    return (grad_q, grad_k, grad_v)


def solution(mesh):
    spec = P(("dp", "seq"), None)
    return jax.shard_map(
        local,
        mesh=mesh,
        in_specs=(spec, spec, spec, spec, P()),
        out_specs=(spec, spec, spec),
        check_vma=False,
    )
```

```python
import functools

import jax
import jax.numpy as jnp
from jax import lax
from jax.experimental import pallas as pl
from jax.experimental.pallas import tpu as pltpu
from jax.sharding import PartitionSpec as P

QH = 32
KVH = 4
HD = 128
PER_KV = QH // KVH
LOG2E = 1.4426950408889634
NT = (((1,), (1,)), ((), ()))
NN = (((1,), (0,)), ((), ()))
TN = (((0,), (0,)), ((), ()))


def dot(a, b, dims):
    return lax.dot_general(a, b, dims, preferred_element_type=jnp.float32)


def distance(pair, k, pairs):
    return lax.rem(pair - (pair ^ k) + pairs, pairs)


def attend_kernel(g, seq_count, info_ref, doc_ref, q_mine, o_mine, qo_theirs, *refs):
    pairs = seq_count // 2
    kv_refs = refs[: pairs + 1]
    dq_mine, dq_theirs, own_out = refs[pairs + 1 : pairs + 4]
    part_outs = refs[pairs + 4 : 2 * pairs + 4]
    kv_all, prob_s, dprob_s, peak_s, stat_s, dq_s, dkv_s = refs[2 * pairs + 4 :]
    tok = q_mine.shape[0]
    keys = 2 * tok
    lanes = PER_KV * tok
    width = lanes // tok * HD
    inv_root = HD ** -0.5
    seq_idx = info_ref[1]
    core = lax.rem(seq_idx, 2)
    pair = seq_idx // 2
    chip = info_ref[0] * pairs + pair

    kv_all[0] = kv_refs[0][...]
    kv_all[pairs] = kv_refs[pairs][...]
    for k in range(1, pairs):
        kv_all[distance(pair, k, pairs)] = kv_refs[k][...]
    dkv_s[...] = jnp.zeros_like(dkv_s)
    dq_s[...] = jnp.zeros_like(dq_s)
    stat_s[0] = jnp.full_like(stat_s[0], -1e30)
    stat_s[1] = jnp.zeros_like(stat_s[1])
    stat_s[2] = jnp.zeros_like(stat_s[2])

    row = lax.broadcasted_iota(jnp.int32, (keys, tok), 0)
    row = ((row // tok) ^ core) * tok + lax.rem(row, tok)
    first = chip * keys
    pos = [
        first + (core ^ half) * tok + lax.broadcasted_iota(jnp.int32, (1, tok), 1)
        for half in range(2)
    ]
    starts = [jnp.zeros_like(p) for p in pos]
    low = first * 0
    end = first * 0
    for d in range(doc_ref.shape[0]):
        end = end + doc_ref[d]
        low = jnp.where(first >= end, end, low)
        starts = [jnp.where(p >= end, end, s) for p, s in zip(pos, starts)]
    count = chip - low // keys + 1

    def pieces():
        for half in range(2):
            for c in range(PER_KV // 2):
                yield half, c, pl.ds(half * lanes + c * keys, keys)

    def rows_of(ref, offset, c):
        return jnp.concatenate(
            [ref[:, pl.ds(offset + (2 * c + i) * HD, HD)] for i in range(2)], 0
        )

    mine_at = pl.multiple_of((core * (KVH // 2) + g) * width, HD)

    def q_rows(half, c):
        return rows_of(q_mine, mine_at, c) if half == 0 else rows_of(qo_theirs.at[0], g * width, c)

    def o_rows(half, c):
        return rows_of(o_mine, mine_at, c) if half == 0 else rows_of(qo_theirs.at[1], g * width, c)

    def stat_step(back, carry):
        k_tile = kv_all[back, :, pl.ds(0, HD)]
        v_tile = kv_all[back, :, pl.ds(HD, HD)]
        key_pos = (chip - back) * keys + row
        biases = []
        for half in range(2):
            bias = jnp.where((key_pos >= starts[half]) & (key_pos <= pos[half]), 0.0, -1e30)
            biases.append(jnp.concatenate([bias, bias], 1))
        for half, c, cols in pieces():
            peak = stat_s[0, :, cols]
            scores = dot(k_tile, q_rows(half, c), NT) * (inv_root * LOG2E) + biases[half]
            dprobs = dot(v_tile, o_rows(half, c), NT)
            new_peak = jnp.maximum(peak, jnp.max(scores, 0, keepdims=True))
            weights = jnp.exp2(scores - new_peak)
            rescale = jnp.exp2(peak - new_peak)
            stat_s[0, :, cols] = new_peak
            stat_s[1, :, cols] = stat_s[1, :, cols] * rescale + jnp.sum(weights, 0, keepdims=True)
            stat_s[2, :, cols] = stat_s[2, :, cols] * rescale + jnp.sum(
                weights * dprobs, 0, keepdims=True
            )
            prob_s[back, :, cols] = weights
            dprob_s[back, :, cols] = dprobs
            peak_s[back, :, cols] = new_peak
        return carry

    lax.fori_loop(0, count, stat_step, 0)
    inv_total = 1.0 / stat_s[1]
    stat_s[1] = inv_total
    stat_s[2] = stat_s[2] * inv_total

    def grad_step(back, carry):
        k_tile = kv_all[back, :, pl.ds(0, HD)]
        dk = jnp.zeros((keys, HD), jnp.float32)
        dv = jnp.zeros((keys, HD), jnp.float32)
        for half, c, cols in pieces():
            factor = jnp.exp2(peak_s[back, :, cols] - stat_s[0, :, cols]) * stat_s[1, :, cols]
            probs = prob_s[back, :, cols] * factor
            probs_b = probs.astype(jnp.bfloat16)
            dscores = (probs * (dprob_s[back, :, cols] - stat_s[2, :, cols])).astype(jnp.bfloat16)
            dv = dv + dot(probs_b, o_rows(half, c), NN)
            dk = dk + dot(dscores, q_rows(half, c), NN)
            dq_s[:, cols] += dot(k_tile, dscores, TN)
        dkv_s[back, :, pl.ds(0, HD)] = dk * inv_root
        dkv_s[back, :, pl.ds(HD, HD)] = dv
        return carry

    lax.fori_loop(0, count, grad_step, 0)
    own_out[...] = dkv_s[0]
    part_outs[pairs - 1][...] = dkv_s[pairs].astype(jnp.bfloat16)
    for k in range(1, pairs):
        part_outs[k - 1][...] = dkv_s[distance(pair, k, pairs)].astype(jnp.bfloat16)
    for half, dq_ref in enumerate((dq_mine, dq_theirs)):
        for h in range(PER_KV):
            block = dq_s[:, pl.ds(half * lanes + h * tok, tok)] * inv_root
            dq_ref[:, pl.ds(h * HD, HD)] = block.T.astype(jnp.bfloat16)


def attend(g, info, doc_lengths, queries, grad_out, qo_theirs, blocks, seq_count):
    tok = queries.shape[0]
    pairs = seq_count // 2
    lanes = PER_KV * tok
    keys, cols = blocks[0].shape
    width = PER_KV * HD
    dq_shape = jax.ShapeDtypeStruct((tok, width), jnp.bfloat16)
    part = jax.ShapeDtypeStruct((keys, cols), jnp.bfloat16)
    out_shape = [dq_shape, dq_shape, jax.ShapeDtypeStruct((keys, cols), jnp.float32)] + [part] * pairs
    smem = pl.BlockSpec(memory_space=pltpu.SMEM)
    vmem = pl.BlockSpec(memory_space=pltpu.VMEM)
    slots = pairs + 1
    scratch = 8 * slots * keys * 2 * lanes + 4 * HD * 2 * lanes + 10 * slots * keys * cols
    operands = 12 * tok * QH * HD + 8 * slots * keys * cols
    return pl.pallas_call(
        functools.partial(attend_kernel, g, seq_count),
        out_shape=out_shape,
        in_specs=[smem, smem] + [vmem] * (3 + len(blocks)),
        out_specs=[vmem] * len(out_shape),
        scratch_shapes=[
            pltpu.VMEM((slots, keys, cols), jnp.bfloat16),
            pltpu.VMEM((slots, keys, 2 * lanes), jnp.float32),
            pltpu.VMEM((slots, keys, 2 * lanes), jnp.float32),
            pltpu.VMEM((slots, 1, 2 * lanes), jnp.float32),
            pltpu.VMEM((3, 1, 2 * lanes), jnp.float32),
            pltpu.VMEM((HD, 2 * lanes), jnp.float32),
            pltpu.VMEM((slots, keys, cols), jnp.float32),
        ],
        compiler_params=pltpu.CompilerParams(vmem_limit_bytes=scratch + operands + 4 * 1024 * 1024),
        cost_estimate=pl.CostEstimate(
            flops=10 * keys * 2 * lanes * HD * (pairs + 1),
            bytes_accessed=8 * 1024 * 1024,
            transcendentals=keys * 2 * lanes * (pairs + 1),
        ),
        name="attend_%d" % g,
    )(info, doc_lengths, queries, grad_out, qo_theirs, *blocks)


def local(queries, keys, values, grad_out, doc_lengths):
    tok = queries.shape[0]
    dp_count = lax.axis_size("dp")
    seq_count = lax.axis_size("seq")
    pairs = seq_count // 2
    dp_idx = lax.axis_index("dp")
    seq_idx = lax.axis_index("seq")
    core = lax.rem(seq_idx, 2)
    pair = seq_idx // 2
    groups = KVH // 2

    def swap(value, k):
        return lax.ppermute(value, "seq", [(i, i ^ k) for i in range(seq_count)])

    def kv_half(which):
        return [
            jnp.concatenate(
                [
                    lax.dynamic_slice_in_dim(t, (which * groups + g) * HD, HD, 1)
                    for t in (keys, values)
                ],
                1,
            )
            for g in range(groups)
        ]

    received = swap(jnp.stack(kv_half(1 - core)), 1)
    own = [jnp.concatenate([m, received[g]], 0) for g, m in enumerate(kv_half(core))]
    prev = [
        lax.ppermute(o, "dp", [(i, i + 1) for i in range(dp_count - 1)]) for o in own
    ]
    width = QH // 2 * HD
    qo_theirs = swap(
        jnp.stack(
            [lax.dynamic_slice_in_dim(t, (1 - core) * width, width, 1) for t in (queries, grad_out)]
        ),
        1,
    )
    info = jnp.stack([dp_idx, seq_idx]).astype(jnp.int32)

    blocks = []
    for g in range(groups):
        sent = [swap(jnp.where((pair ^ k) > pair, own[g], prev[g]), 2 * k) for k in range(1, pairs)]
        blocks.append([own[g]] + sent + [prev[g]])
    dq_mine, dq_other, totals = [], [], []
    for g in range(groups):
        outs = attend(g, info, doc_lengths, queries, grad_out, qo_theirs, blocks[g], seq_count)
        dq_mine.append(outs[0])
        dq_other.append(swap(outs[1], 1))
        own_sum = outs[2]
        prev_sum = outs[-1].astype(jnp.float32)
        for k in range(1, pairs):
            back = swap(outs[2 + k], 2 * k).astype(jnp.float32)
            later = (pair ^ k) > pair
            own_sum = own_sum + jnp.where(later, back, 0.0)
            prev_sum = prev_sum + jnp.where(later, 0.0, back)
        from_next = lax.ppermute(
            prev_sum.astype(jnp.bfloat16), "dp", [(i + 1, i) for i in range(dp_count - 1)]
        )
        totals.append((own_sum + from_next.astype(jnp.float32)).astype(jnp.bfloat16))
    mine = [t[:tok] for t in totals]
    other = [swap(t[tok:], 1) for t in totals]

    def join(a, b):
        low = [jnp.where(core == 0, x, y) for x, y in zip(a, b)]
        high = [jnp.where(core == 0, y, x) for x, y in zip(a, b)]
        return jnp.concatenate(low + high, 1)

    grad_q = join(dq_mine, dq_other)
    grad_k = join([m[:, :HD] for m in mine], [o[:, :HD] for o in other])
    grad_v = join([m[:, HD:] for m in mine], [o[:, HD:] for o in other])
    return (grad_q, grad_k, grad_v)


def solution(mesh):
    spec = P(("dp", "seq"), None)
    return jax.shard_map(
        local,
        mesh=mesh,
        in_specs=(spec, spec, spec, spec, P()),
        out_specs=(spec, spec, spec),
        check_vma=False,
    )
```

```python
import functools

import jax
import jax.numpy as jnp
from jax import lax
from jax.experimental import pallas as pl
from jax.experimental.pallas import tpu as pltpu
from jax.sharding import PartitionSpec as P

QH = 32
KVH = 4
HD = 128
PER_KV = QH // KVH
GROUPS = KVH // 2
MIB = 1024 * 1024
INV_ROOT = HD ** -0.5
TO_LOG2 = INV_ROOT * 1.4426950408889634
NT = (((1,), (1,)), ((), ()))
NN = (((1,), (0,)), ((), ()))
TN = (((0,), (0,)), ((), ()))
K_COLS = pl.ds(0, HD)
V_COLS = pl.ds(HD, HD)


def dot(a, b, dims):
    return lax.dot_general(a, b, dims, preferred_element_type=jnp.float32)


def distance(pair, k, pairs):
    return lax.rem(pair - (pair ^ k) + pairs, pairs)


def place(info_ref, doc_ref, tok, pairs):
    core = lax.rem(info_ref[1], 2)
    chip = info_ref[0] * pairs + info_ref[1] // 2
    first = chip * 2 * tok
    pos = [
        first + (core ^ half) * tok + lax.broadcasted_iota(jnp.int32, (1, tok), 1)
        for half in range(2)
    ]
    starts = [jnp.zeros_like(p) for p in pos]
    low = first * 0
    end = first * 0
    for d in range(doc_ref.shape[0]):
        end = end + doc_ref[d]
        low = jnp.where(first >= end, end, low)
        starts = [jnp.where(p >= end, end, s) for p, s in zip(pos, starts)]
    return core, chip, pos, starts, chip - low // (2 * tok) + 1


def key_rows(core, tok):
    row = lax.broadcasted_iota(jnp.int32, (2 * tok, tok), 0)
    return ((row // tok) ^ core) * tok + lax.rem(row, tok)


def pieces(tok):
    for half in range(2):
        for c in range(PER_KV // 2):
            yield half, pl.ds(c * 2 * tok, 2 * tok), pl.ds((half * PER_KV + 2 * c) * tok, 2 * tok)


def softmax_step(k_tile, v_tile, q_rows, o_rows, bias, peak):
    scores = dot(k_tile, q_rows, NT) * TO_LOG2 + bias
    dprobs = dot(v_tile, o_rows, NT)
    top = jnp.max(scores, 0, keepdims=True)
    new_peak = top if peak is None else jnp.maximum(peak, top)
    weights = jnp.exp2(scores - new_peak)
    total = jnp.sum(weights, 0, keepdims=True)
    mixed = jnp.sum(weights * dprobs, 0, keepdims=True)
    return weights, dprobs, new_peak, total, mixed


def grad_terms(weights, dprobs, peak, stat_ref, cols):
    factor = jnp.exp2(peak - stat_ref[0:1, cols]) * stat_ref[1:2, cols]
    probs = weights * factor
    dscores = probs * (dprobs - stat_ref[2:3, cols])
    return probs.astype(jnp.bfloat16), dscores.astype(jnp.bfloat16)


def own_kernel(pairs, info_ref, doc_ref, *refs):
    blocks = refs[:GROUPS]
    sides = (refs[GROUPS : GROUPS + 2], refs[GROUPS + 2 : GROUPS + 4])
    qo_ref, kept_ref, stat_out, sems = refs[GROUPS + 4 :]
    tok = blocks[0].shape[0] // 2
    width = PER_KV * HD
    core, chip, pos, starts, _ = place(info_ref, doc_ref, tok, pairs)
    key_pos = chip * 2 * tok + key_rows(core, tok)
    biases = []
    for half in range(2):
        bias = jnp.where((key_pos >= starts[half]) & (key_pos <= pos[half]), 0.0, -1e30)
        biases.append(jnp.concatenate([bias, bias], 1))
    mine_at = pl.multiple_of(core * GROUPS * width, HD)
    def slab(g, i, half, h):
        return pltpu.make_async_copy(
            sides[half][i].at[:, pl.ds(pl.multiple_of(mine_at + (g * PER_KV + h) * HD, HD), HD)],
            qo_ref.at[g, i, half, pl.ds(h * tok, tok), :],
            sems.at[g, i, half, h],
        )

    slabs = [
        (g, i, half, h)
        for g in range(GROUPS)
        for half in range(2)
        for h in range(PER_KV)
        for i in range(2)
    ]
    for at in slabs:
        slab(*at).start()
    for g in range(GROUPS):
        k_tile = blocks[g][:, K_COLS]
        v_tile = blocks[g][:, V_COLS]
        for half, rows, cols in pieces(tok):
            if rows.start == 0:
                for at in slabs:
                    if at[0] == g and at[2] == half:
                        slab(*at).wait()
            weights, dprobs, peak, total, mixed = softmax_step(
                k_tile, v_tile, qo_ref[g, 0, half, rows, :], qo_ref[g, 1, half, rows, :], biases[half], None
            )
            kept_ref[g, 0, :, cols] = weights
            kept_ref[g, 1, :, cols] = dprobs
            stat_out[g, 0:1, cols] = peak
            stat_out[g, 1:2, cols] = total
            stat_out[g, 2:3, cols] = mixed


def reach_kernel(g, pairs, info_ref, doc_ref, qo_ref, first_stat, *refs):
    kv_refs = refs[: pairs + 1]
    refs = refs[-(2 * pairs + 3 + 4 - pairs) :]
    part_outs = refs[:pairs]
    ds_out, kv_all, stat_ref, weight_s, dprob_s, peak_s, dkv_s = refs[pairs:]
    keys = kv_refs[0].shape[0]
    tok = keys // 2
    pair = info_ref[1] // 2
    core, chip, _, starts, count = place(info_ref, doc_ref, tok, pairs)

    kv_all[0] = kv_refs[0][...]
    kv_all[pairs] = kv_refs[pairs][...]
    for k in range(1, pairs):
        kv_all[distance(pair, k, pairs)] = kv_refs[k][...]
    dkv_s[...] = jnp.zeros_like(dkv_s)
    stat_ref[...] = first_stat[g]
    row = key_rows(core, tok)

    def stat_step(back, carry):
        k_tile = kv_all[back, :, K_COLS]
        v_tile = kv_all[back, :, V_COLS]
        key_pos = (chip - back) * keys + row
        biases = []
        for half in range(2):
            bias = jnp.where(key_pos >= starts[half], 0.0, -1e30)
            biases.append(jnp.concatenate([bias, bias], 1))
        for half, rows, cols in pieces(tok):
            old = stat_ref[0:1, cols]
            weights, dprobs, peak, total, mixed = softmax_step(
                k_tile, v_tile, qo_ref[g, 0, half, rows, :], qo_ref[g, 1, half, rows, :], biases[half], old
            )
            rescale = jnp.exp2(old - peak)
            stat_ref[0:1, cols] = peak
            stat_ref[1:2, cols] = stat_ref[1:2, cols] * rescale + total
            stat_ref[2:3, cols] = stat_ref[2:3, cols] * rescale + mixed
            weight_s[back - 1, :, cols] = weights
            dprob_s[back - 1, :, cols] = dprobs
            peak_s[back - 1, :, cols] = peak
        return carry

    lax.fori_loop(1, count, stat_step, 0)
    inv_total = 1.0 / stat_ref[1:2, :]
    stat_ref[1:2, :] = inv_total
    stat_ref[2:3, :] = stat_ref[2:3, :] * inv_total

    def grad_step(back, carry):
        dk = jnp.zeros((keys, HD), jnp.float32)
        dv = jnp.zeros((keys, HD), jnp.float32)
        for half, rows, cols in pieces(tok):
            probs_b, dscores = grad_terms(
                weight_s[back - 1, :, cols],
                dprob_s[back - 1, :, cols],
                peak_s[back - 1, :, cols],
                stat_ref,
                cols,
            )
            dv = dv + dot(probs_b, qo_ref[g, 1, half, rows, :], NN)
            dk = dk + dot(dscores, qo_ref[g, 0, half, rows, :], NN)
            ds_out[back - 1, :, cols] = dscores
        dkv_s[back - 1, :, K_COLS] = (dk * INV_ROOT).astype(jnp.bfloat16)
        dkv_s[back - 1, :, V_COLS] = dv.astype(jnp.bfloat16)
        return carry

    lax.fori_loop(1, count, grad_step, 0)
    part_outs[pairs - 1][...] = dkv_s[pairs - 1]
    for k in range(1, pairs):
        part_outs[k - 1][...] = dkv_s[distance(pair, k, pairs) - 1]


def rest_kernel(
    g, pairs, info_ref, doc_ref, qo_ref, kept_ref, first_stat, stat_ref, ds_ref, kv_ref, *refs
):
    own_out, dq_mine, dq_theirs, dq_s = refs[-4:]
    keys = kv_ref.shape[1]
    tok = keys // 2
    count = place(info_ref, doc_ref, tok, pairs)[-1]
    k_tile = kv_ref[0, :, K_COLS]
    dk = jnp.zeros((keys, HD), jnp.float32)
    dv = jnp.zeros((keys, HD), jnp.float32)
    for half, rows, cols in pieces(tok):
        probs_b, dscores = grad_terms(
            kept_ref[g, 0, :, cols], kept_ref[g, 1, :, cols], first_stat[g, 0:1, cols], stat_ref, cols
        )
        dv = dv + dot(probs_b, qo_ref[g, 1, half, rows, :], NN)
        dk = dk + dot(dscores, qo_ref[g, 0, half, rows, :], NN)
        dq_s[:, cols] = dot(k_tile, dscores, TN)
    own_out[:, K_COLS] = dk * INV_ROOT
    own_out[:, V_COLS] = dv

    def query_step(back, carry):
        k_tile = kv_ref[back, :, K_COLS]
        for half, rows, cols in pieces(tok):
            dq_s[:, cols] += dot(k_tile, ds_ref[back - 1, :, cols], TN)
        return carry

    lax.fori_loop(1, count, query_step, 0)
    for half, dq_ref in enumerate((dq_mine, dq_theirs)):
        for h in range(PER_KV):
            block = dq_s[:, pl.ds((half * PER_KV + h) * tok, tok)] * INV_ROOT
            dq_ref[:, pl.ds(h * HD, HD)] = block.T.astype(jnp.bfloat16)


def finish_kernel(tok, info_ref, *refs):
    own = refs[:GROUPS]
    back = refs[GROUPS : 2 * GROUPS]
    own_other = refs[2 * GROUPS]
    back_other = refs[2 * GROUPS + 1 : 3 * GROUPS + 1]
    grad_k, grad_v = refs[3 * GROUPS + 1 :]
    core = lax.rem(info_ref[1], 2)
    for g in range(GROUPS):
        mine = own[g][:tok] + back[g][:tok].astype(jnp.float32)
        other = own_other[g] + back_other[g][tok:].astype(jnp.float32)
        for total, side in ((mine, core), (other, 1 - core)):
            cols = pl.ds(pl.multiple_of((side * GROUPS + g) * HD, HD), HD)
            grad_k[:, cols] = total[:, :HD].astype(jnp.bfloat16)
            grad_v[:, cols] = total[:, HD:].astype(jnp.bfloat16)


def nbytes(shapes):
    total = 0
    for s in shapes:
        size = jnp.dtype(s.dtype).itemsize
        for n in s.shape:
            size *= n
        total += size
    return total


def call(kernel, name, scalars, arrays, out_shape, scratch=(), flops=0, passing=(), hbm=(), sems=None):
    smem = pl.BlockSpec(memory_space=pltpu.SMEM)
    vmem = pl.BlockSpec(memory_space=pltpu.VMEM)
    used = nbytes(arrays) + nbytes(out_shape) + nbytes(scratch)
    return pl.pallas_call(
        kernel,
        out_shape=out_shape,
        in_specs=[smem] * len(scalars)
        + [vmem] * len(arrays)
        + [pl.BlockSpec(memory_space=pl.ANY)] * (len(hbm) + len(passing)),
        out_specs=[vmem] * len(out_shape),
        scratch_shapes=[pltpu.VMEM(s.shape, s.dtype) for s in scratch]
        + ([pltpu.SemaphoreType.DMA(sems)] if sems else []),
        compiler_params=pltpu.CompilerParams(vmem_limit_bytes=used + 3 * MIB),
        cost_estimate=pl.CostEstimate(
            flops=flops, bytes_accessed=nbytes(arrays) + nbytes(out_shape), transcendentals=0
        ),
        name=name,
    )(*scalars, *arrays, *(pltpu.with_memory_space_constraint(a, pltpu.HBM) for a in hbm), *passing)


def local(queries, keys, values, grad_out, doc_lengths):
    tok = queries.shape[0]
    dp_count = lax.axis_size("dp")
    seq_count = lax.axis_size("seq")
    pairs = seq_count // 2
    dp_idx = lax.axis_index("dp")
    seq_idx = lax.axis_index("seq")
    core = lax.rem(seq_idx, 2)
    pair = seq_idx // 2
    rows = 2 * tok
    lanes = 2 * PER_KV * tok
    f32, bf16 = jnp.float32, jnp.bfloat16
    shape = jax.ShapeDtypeStruct

    def swap(value, k):
        return lax.ppermute(value, "seq", [(i, i ^ k) for i in range(seq_count)])

    k_theirs = swap(keys, 1)
    v_theirs = swap(values, 1)

    def block(g):
        at = (core * GROUPS + g) * HD
        cut = [
            [lax.dynamic_slice_in_dim(t, at, HD, 1) for t in side]
            for side in ((keys, values), (k_theirs, v_theirs))
        ]
        return jnp.concatenate([jnp.concatenate(side, 1) for side in cut], 0)

    own = [block(g) for g in range(GROUPS)]
    prev = [lax.ppermute(o, "dp", [(i, (i + 1) % dp_count) for i in range(dp_count)]) for o in own]
    q_sent, o_sent, _ = lax.optimization_barrier((queries, grad_out, own[-1]))
    q_theirs, o_theirs = swap(q_sent, 1), swap(o_sent, 1)
    info = jnp.stack([dp_idx, seq_idx]).astype(jnp.int32)
    scalars = [info, doc_lengths]

    blocks = []
    for g in range(GROUPS):
        own_now, prev_now = own[g], prev[g]
        if g:
            own_now, *_ = lax.optimization_barrier((own_now, *chosen))
        chosen = [jnp.where((pair ^ k) > pair, own_now, prev_now) for k in range(1, pairs)]
        sent = [swap(c, 2 * k) for k, c in enumerate(chosen, 1)]
        blocks.append([own[g]] + sent + [prev[g]])

    stat = shape((3, lanes), f32)
    unit = 2 * rows * lanes * HD
    outs = call(
        functools.partial(own_kernel, pairs),
        "own",
        scalars,
        own,
        [
            shape((GROUPS, 2, 2, PER_KV * tok, HD), bf16),
            shape((GROUPS, 2, rows, lanes), f32),
            shape((GROUPS, 3, lanes), f32),
        ],
        flops=2 * GROUPS * unit,
        hbm=[queries, grad_out, q_theirs, o_theirs],
        sems=(GROUPS, 2, 2, PER_KV),
    )
    qo, kept, first_stats = outs

    part = shape((rows, 2 * HD), bf16)
    reached, own_parts = [], []
    for g in range(GROUPS):
        stats = first_stats
        if g:
            stats, _ = lax.optimization_barrier((stats, reached[-1][pairs + 2]))
        reached.append(
            call(
                functools.partial(reach_kernel, g, pairs),
                "reach_%d" % g,
                scalars,
                [qo, stats] + blocks[g],
                [part] * pairs
                + [shape((pairs, rows, lanes), bf16), shape((pairs + 1, rows, 2 * HD), bf16), stat],
                [
                    shape((pairs, rows, lanes), f32),
                    shape((pairs, rows, lanes), f32),
                    shape((pairs, 1, lanes), f32),
                    shape((pairs, rows, 2 * HD), bf16),
                ],
                flops=4 * pairs * unit,
                passing=[kept] + [r[pairs] for r in reached],
            )
        )
    own_sums, backs, marks = [], [], []
    for g in range(GROUPS):
        prev_sum = reached[g][pairs - 1].astype(f32)
        own_sum = 0.0
        received = [swap(reached[g][k - 1], 2 * k) for k in range(1, pairs)]
        for k in range(1, pairs):
            back = received[k - 1].astype(f32)
            later = (pair ^ k) > pair
            own_sum = own_sum + jnp.where(later, back, 0.0)
            prev_sum = prev_sum + jnp.where(later, 0.0, back)
        own_sums.append(own_sum)
        prev_sum = prev_sum.astype(bf16)
        marks.append(prev_sum)
        backs.append(
            lax.ppermute(
                prev_sum, "dp", [((i + 1) % dp_count, i) for i in range(dp_count)]
            )
        )
    dq_mine, dq_other = [], []
    for g in range(GROUPS):
        ds, kv, stats = reached[g][pairs:]
        stats, _ = lax.optimization_barrier((stats, marks[g]))
        dq_shape = shape((tok, PER_KV * HD), bf16)
        own_part, mine, theirs = call(
            functools.partial(rest_kernel, g, pairs),
            "rest_%d" % g,
            scalars,
            [qo, kept, first_stats, stats, ds, kv],
            [shape((rows, 2 * HD), f32), dq_shape, dq_shape],
            [shape((HD, lanes), f32)],
            flops=(3 + pairs) * unit,
            passing=[r[pairs] for r in reached[g + 1 :]],
        )
        own_sums[g] = own_sums[g] + own_part
        dq_mine.append(mine)
        dq_other.append(swap(theirs, 1))
    own_other = swap(jnp.stack([t[tok:] for t in own_sums]), 1)
    low = [jnp.where(core == 0, x, y) for x, y in zip(dq_mine, dq_other)]
    high = [jnp.where(core == 0, y, x) for x, y in zip(dq_mine, dq_other)]
    grad_q = jnp.concatenate(low + high, 1)
    grad_q, own_other, backs[-1] = lax.optimization_barrier((grad_q, own_other, backs[-1]))
    back_other = [swap(b, 1) for b in backs]
    out = shape((tok, KVH * HD), bf16)
    grad_k, grad_v = call(
        functools.partial(finish_kernel, tok),
        "finish",
        [info],
        own_sums + backs + [own_other] + back_other,
        [out, out],
    )
    return (grad_q, grad_k, grad_v)


def solution(mesh):
    spec = P(("dp", "seq"), None)
    return jax.shard_map(
        local,
        mesh=mesh,
        in_specs=(spec, spec, spec, spec, P()),
        out_specs=(spec, spec, spec),
        check_vma=False,
    )
```

```python
import functools

import jax
import jax.numpy as jnp
from jax import lax
from jax.experimental import pallas as pl
from jax.experimental.pallas import tpu as pltpu
from jax.sharding import PartitionSpec as P

QH = 32
KVH = 4
HD = 128
PER_KV = QH // KVH
GROUPS = KVH // 2
MIB = 1024 * 1024
INV_ROOT = HD ** -0.5
TO_LOG2 = INV_ROOT * 1.4426950408889634
NT = (((1,), (1,)), ((), ()))
NN = (((1,), (0,)), ((), ()))
TN = (((0,), (0,)), ((), ()))
K_COLS = pl.ds(0, HD)
V_COLS = pl.ds(HD, HD)


def dot(a, b, dims):
    return lax.dot_general(a, b, dims, preferred_element_type=jnp.float32)


def distance(pair, k, pairs):
    return lax.rem(pair - (pair ^ k) + pairs, pairs)


def place(info_ref, doc_ref, tok, pairs):
    core = lax.rem(info_ref[1], 2)
    chip = info_ref[0] * pairs + info_ref[1] // 2
    first = chip * 2 * tok
    pos = [
        first + (core ^ half) * tok + lax.broadcasted_iota(jnp.int32, (1, tok), 1)
        for half in range(2)
    ]
    starts = [jnp.zeros_like(p) for p in pos]
    lows = [first * 0] * 2
    end = first * 0
    for d in range(doc_ref.shape[0]):
        end = end + doc_ref[d]
        lows = [jnp.where(first + i * tok >= end, end, low) for i, low in enumerate(lows)]
        starts = [jnp.where(p >= end, end, s) for p, s in zip(pos, starts)]
    return core, chip, pos, starts, lows


def blocks_back(chip, low, keys):
    return chip - low // keys + 1


def key_rows(core, tok):
    row = lax.broadcasted_iota(jnp.int32, (2 * tok, tok), 0)
    return ((row // tok) ^ core) * tok + lax.rem(row, tok)


def pieces(tok):
    for half in range(2):
        for c in range(PER_KV // 2):
            yield half, pl.ds(c * 2 * tok, 2 * tok), pl.ds((half * PER_KV + 2 * c) * tok, 2 * tok)


def softmax_step(k_tile, v_tile, q_rows, o_rows, bias, peak):
    scores = dot(k_tile, q_rows, NT) * TO_LOG2 + bias
    dprobs = dot(v_tile, o_rows, NT)
    top = jnp.max(scores, 0, keepdims=True)
    new_peak = top if peak is None else jnp.maximum(peak, top)
    weights = jnp.exp2(scores - new_peak)
    total = jnp.sum(weights, 0, keepdims=True)
    mixed = jnp.sum(weights * dprobs, 0, keepdims=True)
    return weights, dprobs, new_peak, total, mixed


def grad_terms(weights, dprobs, peak, stat_ref, cols):
    factor = jnp.exp2(peak - stat_ref[0:1, cols]) * stat_ref[1:2, cols]
    probs = weights * factor
    dscores = probs * (dprobs - stat_ref[2:3, cols])
    return probs.astype(jnp.bfloat16), dscores.astype(jnp.bfloat16)


def own_kernel(pairs, info_ref, doc_ref, *refs):
    blocks = refs[:GROUPS]
    sides = (refs[GROUPS : GROUPS + 2], refs[GROUPS + 2 : GROUPS + 4])
    qo_ref, kept_ref, stat_out, wide_s, sems = refs[GROUPS + 4 :]
    tok = blocks[0].shape[0] // 2
    width = PER_KV * HD
    core, chip, pos, starts, _ = place(info_ref, doc_ref, tok, pairs)
    key_pos = chip * 2 * tok + key_rows(core, tok)
    biases = []
    for half in range(2):
        bias = jnp.where((key_pos >= starts[half]) & (key_pos <= pos[half]), 0.0, -1e30)
        biases.append(jnp.concatenate([bias, bias], 1))
    mine_at = pl.multiple_of(core * GROUPS * width, HD)
    runs = [(g, half, i) for g in range(GROUPS) for half in range(2) for i in range(2)]

    def wide(g, half, i):
        at = pl.multiple_of(mine_at + g * width, HD)
        return pltpu.make_async_copy(
            sides[half][i].at[:, pl.ds(at, width)], wide_s.at[g, half, i], sems.at[g, half, i]
        )

    for run in runs:
        wide(*run).start()
    for g in range(GROUPS):
        k_tile = blocks[g][:, K_COLS]
        v_tile = blocks[g][:, V_COLS]
        for half, rows, cols in pieces(tok):
            if rows.start == 0:
                for i in range(2):
                    wide(g, half, i).wait()
                    for h in range(PER_KV):
                        qo_ref[g, i, half, pl.ds(h * tok, tok), :] = wide_s[g, half, i, :, pl.ds(h * HD, HD)]
            weights, dprobs, peak, total, mixed = softmax_step(
                k_tile, v_tile, qo_ref[g, 0, half, rows, :], qo_ref[g, 1, half, rows, :], biases[half], None
            )
            kept_ref[g, 0, :, cols] = weights
            kept_ref[g, 1, :, cols] = dprobs
            stat_out[g, 0:1, cols] = peak
            stat_out[g, 1:2, cols] = total
            stat_out[g, 2:3, cols] = mixed


def reach_kernel(g, pairs, info_ref, doc_ref, qo_ref, first_stat, *refs):
    kv_refs = refs[: pairs + 1]
    refs = refs[-(2 * pairs + 3 + 4 - pairs) :]
    part_outs = refs[:pairs]
    ds_out, kv_all, stat_ref, weight_s, dprob_s, peak_s, dkv_s = refs[pairs:]
    keys = kv_refs[0].shape[0]
    tok = keys // 2
    pair = info_ref[1] // 2
    core, chip, _, starts, lows = place(info_ref, doc_ref, tok, pairs)
    count, later_count = (blocks_back(chip, low, keys) for low in lows)
    trim = (count == later_count) & (lax.rem(lows[0], keys) >= tok) & (count > 1)
    both_end = jnp.where(trim, later_count - 1, later_count)
    whole = pl.ds(0, keys)
    late_rows, early_rows = (pl.ds(pl.multiple_of((i ^ core) * tok, tok), tok) for i in (1, 0))
    half_cols = PER_KV * tok
    both = [(half, starts[half], rows, cols) for half, rows, cols in pieces(tok)]
    first_start = jnp.where(core == 0, starts[0], starts[1])
    one = [
        (core, first_start, pl.ds(at, keys), pl.ds(pl.multiple_of(core * half_cols + at, keys), keys))
        for at in range(0, half_cols, keys)
    ]

    kv_all[0] = kv_refs[0][...]
    kv_all[pairs] = kv_refs[pairs][...]
    for k in range(1, pairs):
        kv_all[distance(pair, k, pairs)] = kv_refs[k][...]
    dkv_s[...] = jnp.zeros_like(dkv_s)
    stat_ref[...] = first_stat[g]
    row = key_rows(core, tok)
    late = tok + lax.broadcasted_iota(jnp.int32, (tok, tok), 0)

    def stat_block(back, key_rows_, row_pos, todo):
        k_tile = kv_all[back, key_rows_, K_COLS]
        v_tile = kv_all[back, key_rows_, V_COLS]
        key_pos = (chip - back) * keys + row_pos
        biases = {}
        for half, start, rows, cols in todo:
            if id(start) not in biases:
                bias = jnp.where(key_pos >= start, 0.0, -1e30)
                biases[id(start)] = jnp.concatenate([bias, bias], 1)
            old = stat_ref[0:1, cols]
            weights, dprobs, peak, total, mixed = softmax_step(
                k_tile, v_tile, qo_ref[g, 0, half, rows, :], qo_ref[g, 1, half, rows, :], biases[id(start)], old
            )
            rescale = jnp.exp2(old - peak)
            stat_ref[0:1, cols] = peak
            stat_ref[1:2, cols] = stat_ref[1:2, cols] * rescale + total
            stat_ref[2:3, cols] = stat_ref[2:3, cols] * rescale + mixed
            weight_s[back - 1, key_rows_, cols] = weights
            dprob_s[back - 1, key_rows_, cols] = dprobs
            peak_s[back - 1, :, cols] = peak

    def each(start, end, work):
        def step(back, carry):
            work(back)
            return carry

        lax.fori_loop(start, end, step, 0)

    each(1, both_end, lambda back: stat_block(back, whole, row, both))
    each(later_count, count, lambda back: stat_block(back, whole, row, one))

    @pl.when(trim)
    def _():
        stat_block(count - 1, late_rows, late, both)

    inv_total = 1.0 / stat_ref[1:2, :]
    stat_ref[1:2, :] = inv_total
    stat_ref[2:3, :] = stat_ref[2:3, :] * inv_total

    def grad_block(back, key_rows_, todo):
        dk = jnp.zeros((key_rows_.size, HD), jnp.float32)
        dv = jnp.zeros((key_rows_.size, HD), jnp.float32)
        for half, _, rows, cols in todo:
            probs_b, dscores = grad_terms(
                weight_s[back - 1, key_rows_, cols],
                dprob_s[back - 1, key_rows_, cols],
                peak_s[back - 1, :, cols],
                stat_ref,
                cols,
            )
            dv = dv + dot(probs_b, qo_ref[g, 1, half, rows, :], NN)
            dk = dk + dot(dscores, qo_ref[g, 0, half, rows, :], NN)
            ds_out[back - 1, key_rows_, cols] = dscores
        dkv_s[back - 1, key_rows_, K_COLS] = (dk * INV_ROOT).astype(jnp.bfloat16)
        dkv_s[back - 1, key_rows_, V_COLS] = dv.astype(jnp.bfloat16)

    def one_side(back):
        grad_block(back, whole, one)
        unused = pl.ds(pl.multiple_of((1 - core) * half_cols, half_cols), half_cols)
        ds_out[back - 1, :, unused] = jnp.zeros((keys, half_cols), jnp.bfloat16)

    each(1, both_end, lambda back: grad_block(back, whole, both))
    each(later_count, count, one_side)

    @pl.when(trim)
    def _():
        grad_block(count - 1, late_rows, both)
        ds_out[count - 2, early_rows, :] = jnp.zeros((tok, 2 * half_cols), jnp.bfloat16)

    part_outs[pairs - 1][...] = dkv_s[pairs - 1]
    for k in range(1, pairs):
        part_outs[k - 1][...] = dkv_s[distance(pair, k, pairs) - 1]


def rest_kernel(
    g, pairs, info_ref, doc_ref, qo_ref, kept_ref, first_stat, stat_ref, ds_ref, kv_ref, *refs
):
    own_out, dq_mine, dq_theirs, dq_s = refs[-4:]
    keys = kv_ref.shape[1]
    tok = keys // 2
    _, chip, _, _, lows = place(info_ref, doc_ref, tok, pairs)
    count = blocks_back(chip, lows[0], keys)
    k_tile = kv_ref[0, :, K_COLS]
    dk = jnp.zeros((keys, HD), jnp.float32)
    dv = jnp.zeros((keys, HD), jnp.float32)
    for half, rows, cols in pieces(tok):
        probs_b, dscores = grad_terms(
            kept_ref[g, 0, :, cols], kept_ref[g, 1, :, cols], first_stat[g, 0:1, cols], stat_ref, cols
        )
        dv = dv + dot(probs_b, qo_ref[g, 1, half, rows, :], NN)
        dk = dk + dot(dscores, qo_ref[g, 0, half, rows, :], NN)
        dq_s[:, cols] = dot(k_tile, dscores, TN)
    own_out[:, K_COLS] = dk * INV_ROOT
    own_out[:, V_COLS] = dv

    def query_step(back, carry):
        k_tile = kv_ref[back, :, K_COLS]
        for half, rows, cols in pieces(tok):
            dq_s[:, cols] += dot(k_tile, ds_ref[back - 1, :, cols], TN)
        return carry

    lax.fori_loop(1, count, query_step, 0)
    for half, dq_ref in enumerate((dq_mine, dq_theirs)):
        for h in range(PER_KV):
            block = dq_s[:, pl.ds((half * PER_KV + h) * tok, tok)] * INV_ROOT
            dq_ref[:, pl.ds(h * HD, HD)] = block.T.astype(jnp.bfloat16)


def finish_kernel(tok, info_ref, *refs):
    own = refs[:GROUPS]
    back, own_other, back_other, grad_k, grad_v = refs[GROUPS:]
    core = lax.rem(info_ref[1], 2)
    for g in range(GROUPS):
        mine = own[g][:tok] + back[g, :tok].astype(jnp.float32)
        other = own_other[g] + back_other[g].astype(jnp.float32)
        for total, side in ((mine, core), (other, 1 - core)):
            cols = pl.ds(pl.multiple_of((side * GROUPS + g) * HD, HD), HD)
            grad_k[:, cols] = total[:, :HD].astype(jnp.bfloat16)
            grad_v[:, cols] = total[:, HD:].astype(jnp.bfloat16)


def nbytes(shapes):
    total = 0
    for s in shapes:
        size = jnp.dtype(s.dtype).itemsize
        for n in s.shape:
            size *= n
        total += size
    return total


def call(kernel, name, scalars, arrays, out_shape, scratch=(), flops=0, passing=(), hbm=(), sems=None):
    smem = pl.BlockSpec(memory_space=pltpu.SMEM)
    vmem = pl.BlockSpec(memory_space=pltpu.VMEM)
    used = nbytes(arrays) + nbytes(out_shape) + nbytes(scratch)
    return pl.pallas_call(
        kernel,
        out_shape=out_shape,
        in_specs=[smem] * len(scalars)
        + [vmem] * len(arrays)
        + [pl.BlockSpec(memory_space=pl.ANY)] * (len(hbm) + len(passing)),
        out_specs=[vmem] * len(out_shape),
        scratch_shapes=[pltpu.VMEM(s.shape, s.dtype) for s in scratch]
        + ([pltpu.SemaphoreType.DMA(sems)] if sems else []),
        compiler_params=pltpu.CompilerParams(vmem_limit_bytes=used + 3 * MIB),
        cost_estimate=pl.CostEstimate(
            flops=flops, bytes_accessed=nbytes(arrays) + nbytes(out_shape), transcendentals=0
        ),
        name=name,
    )(*scalars, *arrays, *hbm, *passing)


def local(queries, keys, values, grad_out, doc_lengths):
    tok = queries.shape[0]
    dp_count = lax.axis_size("dp")
    seq_count = lax.axis_size("seq")
    pairs = seq_count // 2
    dp_idx = lax.axis_index("dp")
    seq_idx = lax.axis_index("seq")
    core = lax.rem(seq_idx, 2)
    pair = seq_idx // 2
    rows = 2 * tok
    lanes = 2 * PER_KV * tok
    f32, bf16 = jnp.float32, jnp.bfloat16
    shape = jax.ShapeDtypeStruct

    def swap(value, k):
        return lax.ppermute(value, "seq", [(i, i ^ k) for i in range(seq_count)])

    k_theirs = swap(keys, 1)
    v_theirs = swap(values, 1)

    def block(g):
        at = (core * GROUPS + g) * HD
        cut = [
            [lax.dynamic_slice_in_dim(t, at, HD, 1) for t in side]
            for side in ((keys, values), (k_theirs, v_theirs))
        ]
        return jnp.concatenate([jnp.concatenate(side, 1) for side in cut], 0)

    own = [block(g) for g in range(GROUPS)]
    prev = [lax.ppermute(o, "dp", [(i, (i + 1) % dp_count) for i in range(dp_count)]) for o in own]
    q_sent, o_sent, _ = lax.optimization_barrier((queries, grad_out, own[-1]))
    q_theirs, o_theirs = swap(q_sent, 1), swap(o_sent, 1)
    info = jnp.stack([dp_idx, seq_idx]).astype(jnp.int32)
    scalars = [info, doc_lengths]

    blocks = []
    for g in range(GROUPS):
        own_now, prev_now = own[g], prev[g]
        if g:
            own_now, *_ = lax.optimization_barrier((own_now, *chosen))
        chosen = [jnp.where((pair ^ k) > pair, own_now, prev_now) for k in range(1, pairs)]
        sent = [swap(c, 2 * k) for k, c in enumerate(chosen, 1)]
        blocks.append([own[g]] + sent + [prev[g]])

    stat = shape((3, lanes), f32)
    unit = 2 * rows * lanes * HD
    outs = call(
        functools.partial(own_kernel, pairs),
        "own",
        scalars,
        own,
        [
            shape((GROUPS, 2, 2, PER_KV * tok, HD), bf16),
            shape((GROUPS, 2, rows, lanes), f32),
            shape((GROUPS, 3, lanes), f32),
        ],
        flops=2 * GROUPS * unit,
        hbm=[queries, grad_out, q_theirs, o_theirs],
        scratch=[shape((GROUPS, 2, 2, tok, PER_KV * HD), bf16)],
        sems=(GROUPS, 2, 2),
    )
    qo, kept, first_stats = outs

    part = shape((rows, 2 * HD), bf16)
    reached, own_parts = [], []
    for g in range(GROUPS):
        stats = first_stats
        if g:
            stats, _ = lax.optimization_barrier((stats, reached[-1][pairs + 2]))
        reached.append(
            call(
                functools.partial(reach_kernel, g, pairs),
                "reach_%d" % g,
                scalars,
                [qo, stats] + blocks[g],
                [part] * pairs
                + [shape((pairs, rows, lanes), bf16), shape((pairs + 1, rows, 2 * HD), bf16), stat],
                [
                    shape((pairs, rows, lanes), f32),
                    shape((pairs, rows, lanes), f32),
                    shape((pairs, 1, lanes), f32),
                    shape((pairs, rows, 2 * HD), bf16),
                ],
                flops=4 * pairs * unit,
                passing=[kept] + [r[pairs] for r in reached],
            )
        )
    own_sums, prev_sums, dq_mine, dq_other = [], [], [], []

    def rest(g, after):
        ds, kv, stats = reached[g][pairs:]
        stats, *_ = lax.optimization_barrier((stats, reached[-1][pairs + 2], *after))
        dq_shape = shape((tok, PER_KV * HD), bf16)
        own_part, mine, theirs = call(
            functools.partial(rest_kernel, g, pairs),
            "rest_%d" % g,
            scalars,
            [qo, kept, first_stats, stats, ds, kv],
            [shape((rows, 2 * HD), f32), dq_shape, dq_shape],
            [shape((HD, lanes), f32)],
            flops=(3 + pairs) * unit,
            passing=[r[pairs] for r in reached[g + 1 :]],
        )
        dq_mine.append(mine)
        dq_other.append(swap(theirs, 1))
        return own_part

    own_part = None
    for g in range(GROUPS):
        received = [swap(reached[g][k - 1], 2 * k) for k in range(1, pairs)]
        if g:
            own_part = rest(g - 1, prev_sums[-1:])
            received = lax.optimization_barrier((own_part, *received))[1:]
            own_sums[-1] = own_sums[-1] + own_part
        prev_sum = reached[g][pairs - 1].astype(f32)
        own_sum = 0.0
        for k in range(1, pairs):
            back = received[k - 1].astype(f32)
            later = (pair ^ k) > pair
            own_sum = own_sum + jnp.where(later, back, 0.0)
            prev_sum = prev_sum + jnp.where(later, 0.0, back)
        own_sums.append(own_sum)
        prev_sums.append(prev_sum.astype(bf16))
    prev_all = jnp.stack(prev_sums)
    back = lax.ppermute(prev_all, "dp", [((i + 1) % dp_count, i) for i in range(dp_count)])
    own_sums[-1] = own_sums[-1] + rest(GROUPS - 1, [prev_all])
    own_other = swap(jnp.stack([t[tok:] for t in own_sums]), 1)
    low = [jnp.where(core == 0, x, y) for x, y in zip(dq_mine, dq_other)]
    high = [jnp.where(core == 0, y, x) for x, y in zip(dq_mine, dq_other)]
    grad_q = jnp.concatenate(low + high, 1)
    back_other = swap(back[:, tok:], 1)
    out = shape((tok, KVH * HD), bf16)
    grad_k, grad_v = call(
        functools.partial(finish_kernel, tok),
        "finish",
        [info],
        own_sums + [back, own_other, back_other],
        [out, out],
    )
    return (grad_q, grad_k, grad_v)


def solution(mesh):
    spec = P(("dp", "seq"), None)
    return jax.shard_map(
        local,
        mesh=mesh,
        in_specs=(spec, spec, spec, spec, P()),
        out_specs=(spec, spec, spec),
        check_vma=False,
    )
```

```python
import functools

import jax
import jax.numpy as jnp
from jax import lax
from jax.experimental import pallas as pl
from jax.experimental.pallas import tpu as pltpu
from jax.sharding import PartitionSpec as P

QH = 32
KVH = 4
HD = 128
PER_KV = QH // KVH
GROUPS = KVH // 2
MIB = 1024 * 1024
INV_ROOT = HD ** -0.5
TO_LOG2 = INV_ROOT * 1.4426950408889634
NT = (((1,), (1,)), ((), ()))
NN = (((1,), (0,)), ((), ()))
TN = (((0,), (0,)), ((), ()))
K_COLS = pl.ds(0, HD)
V_COLS = pl.ds(HD, HD)


def dot(a, b, dims):
    return lax.dot_general(a, b, dims, preferred_element_type=jnp.float32)


def distance(pair, k, pairs):
    return lax.rem(pair - (pair ^ k) + pairs, pairs)


def place(info_ref, doc_ref, tok, pairs):
    core = lax.rem(info_ref[1], 2)
    chip = info_ref[0] * pairs + info_ref[1] // 2
    first = chip * 2 * tok
    pos = [
        first + (core ^ half) * tok + lax.broadcasted_iota(jnp.int32, (1, tok), 1)
        for half in range(2)
    ]
    starts = [jnp.zeros_like(p) for p in pos]
    lows = [first * 0] * 2
    end = first * 0
    for d in range(doc_ref.shape[0]):
        end = end + doc_ref[d]
        lows = [jnp.where(first + i * tok >= end, end, low) for i, low in enumerate(lows)]
        starts = [jnp.where(p >= end, end, s) for p, s in zip(pos, starts)]
    return core, chip, pos, starts, lows


def blocks_back(chip, low, keys):
    return chip - low // keys + 1


def key_rows(core, tok):
    row = lax.broadcasted_iota(jnp.int32, (2 * tok, tok), 0)
    return ((row // tok) ^ core) * tok + lax.rem(row, tok)


def pieces(tok):
    for half in range(2):
        for c in range(PER_KV // 2):
            yield half, pl.ds(c * 2 * tok, 2 * tok), pl.ds((half * PER_KV + 2 * c) * tok, 2 * tok)


def softmax_step(k_tile, v_tile, q_rows, o_rows, bias, peak):
    scores = dot(k_tile, q_rows, NT) * TO_LOG2 + bias
    dprobs = dot(v_tile, o_rows, NT)
    top = jnp.max(scores, 0, keepdims=True)
    new_peak = top if peak is None else jnp.maximum(peak, top)
    weights = jnp.exp2(scores - new_peak)
    total = jnp.sum(weights, 0, keepdims=True)
    mixed = jnp.sum(weights * dprobs, 0, keepdims=True)
    return weights, dprobs, new_peak, total, mixed


def grad_terms(weights, dprobs, peak, stat_ref, cols):
    factor = jnp.exp2(peak - stat_ref[0:1, cols]) * stat_ref[1:2, cols]
    probs = weights * factor
    dscores = probs * (dprobs - stat_ref[2:3, cols])
    return probs.astype(jnp.bfloat16), dscores.astype(jnp.bfloat16)


def own_kernel(pairs, info_ref, doc_ref, *refs):
    blocks = refs[:GROUPS]
    sides = (refs[GROUPS : GROUPS + 2], refs[GROUPS + 2 : GROUPS + 4])
    qo_ref, kept_ref, stat_out, wide_s, sems = refs[GROUPS + 4 :]
    tok = blocks[0].shape[0] // 2
    width = PER_KV * HD
    mine_at = pl.multiple_of(lax.rem(info_ref[1], 2) * GROUPS * width, HD)
    runs = [(g, half, i) for g in range(GROUPS) for half in range(2) for i in range(2)]

    def wide(g, half, i):
        at = pl.multiple_of(mine_at + g * width, HD)
        return pltpu.make_async_copy(
            sides[half][i].at[:, pl.ds(at, width)], wide_s.at[g, half, i], sems.at[g, half, i]
        )

    for run in runs:
        wide(*run).start()
    core, chip, pos, starts, _ = place(info_ref, doc_ref, tok, pairs)
    key_pos = chip * 2 * tok + key_rows(core, tok)
    biases = []
    for half in range(2):
        bias = jnp.where((key_pos >= starts[half]) & (key_pos <= pos[half]), 0.0, -1e30)
        biases.append(jnp.concatenate([bias, bias], 1))
    for g in range(GROUPS):
        k_tile = blocks[g][:, K_COLS]
        v_tile = blocks[g][:, V_COLS]
        for half, rows, cols in pieces(tok):
            if rows.start == 0:
                for i in range(2):
                    wide(g, half, i).wait()
                    for h in range(PER_KV):
                        qo_ref[g, i, half, pl.ds(h * tok, tok), :] = wide_s[g, half, i, :, pl.ds(h * HD, HD)]
            weights, dprobs, peak, total, mixed = softmax_step(
                k_tile, v_tile, qo_ref[g, 0, half, rows, :], qo_ref[g, 1, half, rows, :], biases[half], None
            )
            kept_ref[g, 0, :, cols] = weights
            kept_ref[g, 1, :, cols] = dprobs
            stat_out[g, 0:1, cols] = peak
            stat_out[g, 1:2, cols] = total
            stat_out[g, 2:3, cols] = mixed


def reach_kernel(g, pairs, info_ref, doc_ref, qo_ref, first_stat, *refs):
    kv_refs = refs[: pairs + 1]
    refs = refs[-(2 * pairs + 3 + 4 - pairs) :]
    part_outs = refs[:pairs]
    ds_out, kv_all, stat_ref, weight_s, dprob_s, peak_s, dkv_s = refs[pairs:]
    keys = kv_refs[0].shape[0]
    tok = keys // 2
    pair = info_ref[1] // 2
    core, chip, _, starts, lows = place(info_ref, doc_ref, tok, pairs)
    count, later_count = (blocks_back(chip, low, keys) for low in lows)
    trim = (count == later_count) & (lax.rem(lows[0], keys) >= tok) & (count > 1)
    both_end = jnp.where(trim, later_count - 1, later_count)
    whole = pl.ds(0, keys)
    late_rows, early_rows = (pl.ds(pl.multiple_of((i ^ core) * tok, tok), tok) for i in (1, 0))
    half_cols = PER_KV * tok
    both = [(half, starts[half], rows, cols) for half, rows, cols in pieces(tok)]
    first_start = jnp.where(core == 0, starts[0], starts[1])
    one = [
        (core, first_start, pl.ds(at, keys), pl.ds(pl.multiple_of(core * half_cols + at, keys), keys))
        for at in range(0, half_cols, keys)
    ]

    kv_all[0] = kv_refs[0][...]
    kv_all[pairs] = kv_refs[pairs][...]
    for k in range(1, pairs):
        kv_all[distance(pair, k, pairs)] = kv_refs[k][...]
    dkv_s[...] = jnp.zeros_like(dkv_s)
    stat_ref[...] = first_stat[g]
    row = key_rows(core, tok)
    late = tok + lax.broadcasted_iota(jnp.int32, (tok, tok), 0)

    def stat_block(back, key_rows_, row_pos, todo):
        k_tile = kv_all[back, key_rows_, K_COLS]
        v_tile = kv_all[back, key_rows_, V_COLS]
        key_pos = (chip - back) * keys + row_pos
        biases = {}
        for half, start, rows, cols in todo:
            if id(start) not in biases:
                bias = jnp.where(key_pos >= start, 0.0, -1e30)
                biases[id(start)] = jnp.concatenate([bias, bias], 1)
            old = stat_ref[0:1, cols]
            weights, dprobs, peak, total, mixed = softmax_step(
                k_tile, v_tile, qo_ref[g, 0, half, rows, :], qo_ref[g, 1, half, rows, :], biases[id(start)], old
            )
            rescale = jnp.exp2(old - peak)
            stat_ref[0:1, cols] = peak
            stat_ref[1:2, cols] = stat_ref[1:2, cols] * rescale + total
            stat_ref[2:3, cols] = stat_ref[2:3, cols] * rescale + mixed
            weight_s[back - 1, key_rows_, cols] = weights
            dprob_s[back - 1, key_rows_, cols] = dprobs
            peak_s[back - 1, :, cols] = peak

    def each(start, end, work):
        def step(back, carry):
            work(back)
            return carry

        lax.fori_loop(start, end, step, 0)

    each(1, both_end, lambda back: stat_block(back, whole, row, both))
    each(later_count, count, lambda back: stat_block(back, whole, row, one))

    @pl.when(trim)
    def _():
        stat_block(count - 1, late_rows, late, both)

    inv_total = 1.0 / stat_ref[1:2, :]
    stat_ref[1:2, :] = inv_total
    stat_ref[2:3, :] = stat_ref[2:3, :] * inv_total

    def grad_block(back, key_rows_, todo):
        dk = jnp.zeros((key_rows_.size, HD), jnp.float32)
        dv = jnp.zeros((key_rows_.size, HD), jnp.float32)
        for half, _, rows, cols in todo:
            probs_b, dscores = grad_terms(
                weight_s[back - 1, key_rows_, cols],
                dprob_s[back - 1, key_rows_, cols],
                peak_s[back - 1, :, cols],
                stat_ref,
                cols,
            )
            dv = dv + dot(probs_b, qo_ref[g, 1, half, rows, :], NN)
            dk = dk + dot(dscores, qo_ref[g, 0, half, rows, :], NN)
            ds_out[back - 1, key_rows_, cols] = dscores
        dkv_s[back - 1, key_rows_, K_COLS] = (dk * INV_ROOT).astype(jnp.bfloat16)
        dkv_s[back - 1, key_rows_, V_COLS] = dv.astype(jnp.bfloat16)

    def one_side(back):
        grad_block(back, whole, one)
        unused = pl.ds(pl.multiple_of((1 - core) * half_cols, half_cols), half_cols)
        ds_out[back - 1, :, unused] = jnp.zeros((keys, half_cols), jnp.bfloat16)

    each(1, both_end, lambda back: grad_block(back, whole, both))
    each(later_count, count, one_side)

    @pl.when(trim)
    def _():
        grad_block(count - 1, late_rows, both)
        ds_out[count - 2, early_rows, :] = jnp.zeros((tok, 2 * half_cols), jnp.bfloat16)

    part_outs[pairs - 1][...] = dkv_s[pairs - 1]
    for k in range(1, pairs):
        part_outs[k - 1][...] = dkv_s[distance(pair, k, pairs) - 1]


def rest_kernel(
    g, pairs, info_ref, doc_ref, qo_ref, kept_ref, first_stat, stat_ref, ds_ref, kv_ref, *refs
):
    own_out, dq_mine, dq_theirs, dq_s = refs[-4:]
    keys = kv_ref.shape[1]
    tok = keys // 2
    _, chip, _, _, lows = place(info_ref, doc_ref, tok, pairs)
    count = blocks_back(chip, lows[0], keys)
    k_tile = kv_ref[0, :, K_COLS]
    dk = jnp.zeros((keys, HD), jnp.float32)
    dv = jnp.zeros((keys, HD), jnp.float32)
    for half, rows, cols in pieces(tok):
        probs_b, dscores = grad_terms(
            kept_ref[g, 0, :, cols], kept_ref[g, 1, :, cols], first_stat[g, 0:1, cols], stat_ref, cols
        )
        dv = dv + dot(probs_b, qo_ref[g, 1, half, rows, :], NN)
        dk = dk + dot(dscores, qo_ref[g, 0, half, rows, :], NN)
        dq_s[:, cols] = dot(k_tile, dscores, TN)
    own_out[:, K_COLS] = dk * INV_ROOT
    own_out[:, V_COLS] = dv

    def query_step(back, carry):
        k_tile = kv_ref[back, :, K_COLS]
        for half, rows, cols in pieces(tok):
            dq_s[:, cols] += dot(k_tile, ds_ref[back - 1, :, cols], TN)
        return carry

    lax.fori_loop(1, count, query_step, 0)
    for half, dq_ref in enumerate((dq_mine, dq_theirs)):
        for h in range(PER_KV):
            block = dq_s[:, pl.ds((half * PER_KV + h) * tok, tok)] * INV_ROOT
            dq_ref[:, pl.ds(h * HD, HD)] = block.T.astype(jnp.bfloat16)


def finish_kernel(tok, info_ref, *refs):
    own = refs[:GROUPS]
    back = refs[GROUPS : 2 * GROUPS]
    own_other = refs[2 * GROUPS]
    back_other = refs[2 * GROUPS + 1 : 3 * GROUPS + 1]
    grad_k, grad_v = refs[3 * GROUPS + 1 :]
    core = lax.rem(info_ref[1], 2)
    for g in range(GROUPS):
        mine = own[g][:tok] + back[g][:tok].astype(jnp.float32)
        other = own_other[g] + back_other[g][tok:].astype(jnp.float32)
        for total, side in ((mine, core), (other, 1 - core)):
            cols = pl.ds(pl.multiple_of((side * GROUPS + g) * HD, HD), HD)
            grad_k[:, cols] = total[:, :HD].astype(jnp.bfloat16)
            grad_v[:, cols] = total[:, HD:].astype(jnp.bfloat16)


def nbytes(shapes):
    total = 0
    for s in shapes:
        size = jnp.dtype(s.dtype).itemsize
        for n in s.shape:
            size *= n
        total += size
    return total


def call(kernel, name, scalars, arrays, out_shape, scratch=(), flops=0, passing=(), hbm=(), sems=None):
    smem = pl.BlockSpec(memory_space=pltpu.SMEM)
    vmem = pl.BlockSpec(memory_space=pltpu.VMEM)
    used = nbytes(arrays) + nbytes(out_shape) + nbytes(scratch)
    return pl.pallas_call(
        kernel,
        out_shape=out_shape,
        in_specs=[smem] * len(scalars)
        + [vmem] * len(arrays)
        + [pl.BlockSpec(memory_space=pl.ANY)] * (len(hbm) + len(passing)),
        out_specs=[vmem] * len(out_shape),
        scratch_shapes=[pltpu.VMEM(s.shape, s.dtype) for s in scratch]
        + ([pltpu.SemaphoreType.DMA(sems)] if sems else []),
        compiler_params=pltpu.CompilerParams(vmem_limit_bytes=used + 3 * MIB),
        cost_estimate=pl.CostEstimate(
            flops=flops, bytes_accessed=nbytes(arrays) + nbytes(out_shape), transcendentals=0
        ),
        name=name,
    )(*scalars, *arrays, *hbm, *passing)


def local(queries, keys, values, grad_out, doc_lengths):
    tok = queries.shape[0]
    dp_count = lax.axis_size("dp")
    seq_count = lax.axis_size("seq")
    pairs = seq_count // 2
    dp_idx = lax.axis_index("dp")
    seq_idx = lax.axis_index("seq")
    core = lax.rem(seq_idx, 2)
    pair = seq_idx // 2
    rows = 2 * tok
    lanes = 2 * PER_KV * tok
    f32, bf16 = jnp.float32, jnp.bfloat16
    shape = jax.ShapeDtypeStruct

    def swap(value, k):
        return lax.ppermute(value, "seq", [(i, i ^ k) for i in range(seq_count)])

    k_theirs = swap(keys, 1)
    v_theirs = swap(values, 1)

    def block(g):
        at = (core * GROUPS + g) * HD
        cut = [
            [lax.dynamic_slice_in_dim(t, at, HD, 1) for t in side]
            for side in ((keys, values), (k_theirs, v_theirs))
        ]
        return jnp.concatenate([jnp.concatenate(side, 1) for side in cut], 0)

    own = [block(g) for g in range(GROUPS)]
    prev = [lax.ppermute(o, "dp", [(i, (i + 1) % dp_count) for i in range(dp_count)]) for o in own]
    q_sent, o_sent, _ = lax.optimization_barrier((queries, grad_out, own[-1]))
    q_theirs, o_theirs = swap(q_sent, 1), swap(o_sent, 1)
    info = jnp.stack([dp_idx, seq_idx]).astype(jnp.int32)
    scalars = [info, doc_lengths]

    blocks = []
    for g in range(GROUPS):
        own_now, prev_now = own[g], prev[g]
        if g:
            own_now, *_ = lax.optimization_barrier((own_now, *chosen))
        chosen = [jnp.where((pair ^ k) > pair, own_now, prev_now) for k in range(1, pairs)]
        sent = [swap(c, 2 * k) for k, c in enumerate(chosen, 1)]
        blocks.append([own[g]] + sent + [prev[g]])

    stat = shape((3, lanes), f32)
    unit = 2 * rows * lanes * HD
    outs = call(
        functools.partial(own_kernel, pairs),
        "own",
        scalars,
        own,
        [
            shape((GROUPS, 2, 2, PER_KV * tok, HD), bf16),
            shape((GROUPS, 2, rows, lanes), f32),
            shape((GROUPS, 3, lanes), f32),
        ],
        flops=2 * GROUPS * unit,
        hbm=[queries, grad_out, q_theirs, o_theirs],
        scratch=[shape((GROUPS, 2, 2, tok, PER_KV * HD), bf16)],
        sems=(GROUPS, 2, 2),
    )
    qo, kept, first_stats = outs

    part = shape((rows, 2 * HD), bf16)
    reached, own_parts = [], []
    for g in range(GROUPS):
        stats = first_stats
        if g:
            stats, _ = lax.optimization_barrier((stats, reached[-1][pairs + 2]))
        reached.append(
            call(
                functools.partial(reach_kernel, g, pairs),
                "reach_%d" % g,
                scalars,
                [qo, stats] + blocks[g],
                [part] * pairs
                + [shape((pairs, rows, lanes), bf16), shape((pairs + 1, rows, 2 * HD), bf16), stat],
                [
                    shape((pairs, rows, lanes), f32),
                    shape((pairs, rows, lanes), f32),
                    shape((pairs, 1, lanes), f32),
                    shape((pairs, rows, 2 * HD), bf16),
                ],
                flops=4 * pairs * unit,
                passing=[kept] + [r[pairs] for r in reached],
            )
        )
    own_sums, backs, marks = [], [], []
    for g in range(GROUPS):
        prev_sum = reached[g][pairs - 1].astype(f32)
        own_sum = 0.0
        received = [swap(reached[g][k - 1], 2 * k) for k in range(1, pairs)]
        for k in range(1, pairs):
            back = received[k - 1].astype(f32)
            later = (pair ^ k) > pair
            own_sum = own_sum + jnp.where(later, back, 0.0)
            prev_sum = prev_sum + jnp.where(later, 0.0, back)
        own_sums.append(own_sum)
        prev_sum = prev_sum.astype(bf16)
        marks.append(prev_sum)
        backs.append(
            lax.ppermute(
                prev_sum, "dp", [((i + 1) % dp_count, i) for i in range(dp_count)]
            )
        )
    dq_mine, dq_other = [], []
    for g in range(GROUPS):
        ds, kv, stats = reached[g][pairs:]
        stats, _ = lax.optimization_barrier((stats, marks[g]))
        dq_shape = shape((tok, PER_KV * HD), bf16)
        own_part, mine, theirs = call(
            functools.partial(rest_kernel, g, pairs),
            "rest_%d" % g,
            scalars,
            [qo, kept, first_stats, stats, ds, kv],
            [shape((rows, 2 * HD), f32), dq_shape, dq_shape],
            [shape((HD, lanes), f32)],
            flops=(3 + pairs) * unit,
            passing=[r[pairs] for r in reached[g + 1 :]],
        )
        own_sums[g] = own_sums[g] + own_part
        dq_mine.append(mine)
        dq_other.append(swap(theirs, 1))
    own_other = swap(jnp.stack([t[tok:] for t in own_sums]), 1)
    low = [jnp.where(core == 0, x, y) for x, y in zip(dq_mine, dq_other)]
    high = [jnp.where(core == 0, y, x) for x, y in zip(dq_mine, dq_other)]
    grad_q = jnp.concatenate(low + high, 1)
    grad_q, own_other, backs[-1] = lax.optimization_barrier((grad_q, own_other, backs[-1]))
    back_other = [swap(b, 1) for b in backs]
    out = shape((tok, KVH * HD), bf16)
    grad_k, grad_v = call(
        functools.partial(finish_kernel, tok),
        "finish",
        [info],
        own_sums + backs + [own_other] + back_other,
        [out, out],
    )
    return (grad_q, grad_k, grad_v)


def solution(mesh):
    spec = P(("dp", "seq"), None)
    return jax.shard_map(
        local,
        mesh=mesh,
        in_specs=(spec, spec, spec, spec, P()),
        out_specs=(spec, spec, spec),
        check_vma=False,
    )
```

```python
import functools

import jax
import jax.numpy as jnp
from jax import lax
from jax.experimental import pallas as pl
from jax.experimental.pallas import tpu as pltpu
from jax.sharding import PartitionSpec as P

QH = 32
KVH = 4
HD = 128
PER_KV = QH // KVH
GROUPS = KVH // 2
MIB = 1024 * 1024
INV_ROOT = HD ** -0.5
TO_LOG2 = INV_ROOT * 1.4426950408889634
NT = (((1,), (1,)), ((), ()))
NN = (((1,), (0,)), ((), ()))
TN = (((0,), (0,)), ((), ()))
K_COLS = pl.ds(0, HD)
V_COLS = pl.ds(HD, HD)


def dot(a, b, dims):
    return lax.dot_general(a, b, dims, preferred_element_type=jnp.float32)


def distance(pair, k, pairs):
    return lax.rem(pair - (pair ^ k) + pairs, pairs)


def place(info_ref, doc_ref, tok, pairs):
    core = lax.rem(info_ref[1], 2)
    chip = info_ref[0] * pairs + info_ref[1] // 2
    first = chip * 2 * tok
    pos = [
        first + (core ^ half) * tok + lax.broadcasted_iota(jnp.int32, (1, tok), 1)
        for half in range(2)
    ]
    starts = [jnp.zeros_like(p) for p in pos]
    lows = [first * 0] * 2
    end = first * 0
    for d in range(doc_ref.shape[0]):
        end = end + doc_ref[d]
        lows = [jnp.where(first + i * tok >= end, end, low) for i, low in enumerate(lows)]
        starts = [jnp.where(p >= end, end, s) for p, s in zip(pos, starts)]
    return core, chip, pos, starts, lows


def blocks_back(chip, low, keys):
    return chip - low // keys + 1


def key_rows(core, tok):
    row = lax.broadcasted_iota(jnp.int32, (2 * tok, tok), 0)
    return ((row // tok) ^ core) * tok + lax.rem(row, tok)


def pieces(tok):
    for half in range(2):
        for c in range(PER_KV // 2):
            yield half, pl.ds(c * 2 * tok, 2 * tok), pl.ds((half * PER_KV + 2 * c) * tok, 2 * tok)


def softmax_step(k_tile, v_tile, q_rows, o_rows, bias, peak):
    scores = dot(k_tile, q_rows, NT) * TO_LOG2 + bias
    dprobs = dot(v_tile, o_rows, NT)
    top = jnp.max(scores, 0, keepdims=True)
    new_peak = top if peak is None else jnp.maximum(peak, top)
    weights = jnp.exp2(scores - new_peak)
    total = jnp.sum(weights, 0, keepdims=True)
    mixed = jnp.sum(weights * dprobs, 0, keepdims=True)
    return weights, dprobs, new_peak, total, mixed


def grad_terms(weights, dprobs, peak, stat_ref, cols):
    factor = jnp.exp2(peak - stat_ref[0:1, cols]) * stat_ref[1:2, cols]
    probs = weights * factor
    dscores = probs * (dprobs - stat_ref[2:3, cols])
    return probs.astype(jnp.bfloat16), dscores.astype(jnp.bfloat16)


def own_kernel(pairs, info_ref, doc_ref, *refs):
    blocks = refs[:GROUPS]
    sides = (refs[GROUPS : GROUPS + 2], refs[GROUPS + 2 : GROUPS + 4])
    qo_ref, kept_ref, stat_out, wide_s, sems = refs[GROUPS + 4 :]
    tok = blocks[0].shape[0] // 2
    width = PER_KV * HD
    mine_at = pl.multiple_of(lax.rem(info_ref[1], 2) * GROUPS * width, HD)
    runs = [(g, half, i) for g in range(GROUPS) for half in range(2) for i in range(2)]

    def wide(g, half, i):
        at = pl.multiple_of(mine_at + g * width, HD)
        return pltpu.make_async_copy(
            sides[half][i].at[:, pl.ds(at, width)], wide_s.at[g, half, i], sems.at[g, half, i]
        )

    for run in runs:
        wide(*run).start()
    core, chip, pos, starts, _ = place(info_ref, doc_ref, tok, pairs)
    key_pos = chip * 2 * tok + key_rows(core, tok)
    biases = []
    for half in range(2):
        bias = jnp.where((key_pos >= starts[half]) & (key_pos <= pos[half]), 0.0, -1e30)
        biases.append(jnp.concatenate([bias, bias], 1))
    for g in range(GROUPS):
        k_tile = blocks[g][:, K_COLS]
        v_tile = blocks[g][:, V_COLS]
        for half, rows, cols in pieces(tok):
            if rows.start == 0:
                for i in range(2):
                    wide(g, half, i).wait()
                    for h in range(PER_KV):
                        qo_ref[g, i, half, pl.ds(h * tok, tok), :] = wide_s[g, half, i, :, pl.ds(h * HD, HD)]
            weights, dprobs, peak, total, mixed = softmax_step(
                k_tile, v_tile, qo_ref[g, 0, half, rows, :], qo_ref[g, 1, half, rows, :], biases[half], None
            )
            kept_ref[g, 0, :, cols] = weights
            kept_ref[g, 1, :, cols] = dprobs
            stat_out[g, 0:1, cols] = peak
            stat_out[g, 1:2, cols] = total
            stat_out[g, 2:3, cols] = mixed


def reach_kernel(g, pairs, info_ref, doc_ref, qo_ref, first_stat, *refs):
    kv_refs = refs[: pairs + 1]
    refs = refs[-(2 * pairs + 3 + 4 - pairs) :]
    part_outs = refs[:pairs]
    ds_out, kv_all, stat_ref, weight_s, dprob_s, peak_s, dkv_s = refs[pairs:]
    keys = kv_refs[0].shape[0]
    tok = keys // 2
    pair = info_ref[1] // 2
    core, chip, _, starts, lows = place(info_ref, doc_ref, tok, pairs)
    count, later_count = (blocks_back(chip, low, keys) for low in lows)
    trim = (count == later_count) & (lax.rem(lows[0], keys) >= tok) & (count > 1)
    both_end = jnp.where(trim, later_count - 1, later_count)
    whole = pl.ds(0, keys)
    late_rows, early_rows = (pl.ds(pl.multiple_of((i ^ core) * tok, tok), tok) for i in (1, 0))
    half_cols = PER_KV * tok
    both = [(half, starts[half], rows, cols) for half, rows, cols in pieces(tok)]
    first_start = jnp.where(core == 0, starts[0], starts[1])
    one = [
        (core, first_start, pl.ds(at, keys), pl.ds(pl.multiple_of(core * half_cols + at, keys), keys))
        for at in range(0, half_cols, keys)
    ]

    kv_all[0] = kv_refs[0][...]
    kv_all[pairs] = kv_refs[pairs][...]
    for k in range(1, pairs):
        kv_all[distance(pair, k, pairs)] = kv_refs[k][...]
    dkv_s[...] = jnp.zeros_like(dkv_s)
    stat_ref[...] = first_stat[g]
    row = key_rows(core, tok)
    late = tok + lax.broadcasted_iota(jnp.int32, (tok, tok), 0)

    def stat_block(back, key_rows_, row_pos, todo):
        k_tile = kv_all[back, key_rows_, K_COLS]
        v_tile = kv_all[back, key_rows_, V_COLS]
        key_pos = (chip - back) * keys + row_pos
        biases = {}
        for half, start, rows, cols in todo:
            if id(start) not in biases:
                bias = jnp.where(key_pos >= start, 0.0, -1e30)
                biases[id(start)] = jnp.concatenate([bias, bias], 1)
            old = stat_ref[0:1, cols]
            weights, dprobs, peak, total, mixed = softmax_step(
                k_tile, v_tile, qo_ref[g, 0, half, rows, :], qo_ref[g, 1, half, rows, :], biases[id(start)], old
            )
            rescale = jnp.exp2(old - peak)
            stat_ref[0:1, cols] = peak
            stat_ref[1:2, cols] = stat_ref[1:2, cols] * rescale + total
            stat_ref[2:3, cols] = stat_ref[2:3, cols] * rescale + mixed
            weight_s[back - 1, key_rows_, cols] = weights
            dprob_s[back - 1, key_rows_, cols] = dprobs
            peak_s[back - 1, :, cols] = peak

    def each(start, end, work):
        def step(back, carry):
            work(back)
            return carry

        lax.fori_loop(start, end, step, 0)

    each(1, both_end, lambda back: stat_block(back, whole, row, both))
    each(later_count, count, lambda back: stat_block(back, whole, row, one))

    @pl.when(trim)
    def _():
        stat_block(count - 1, late_rows, late, both)

    inv_total = 1.0 / stat_ref[1:2, :]
    stat_ref[1:2, :] = inv_total
    stat_ref[2:3, :] = stat_ref[2:3, :] * inv_total

    def grad_block(back, key_rows_, todo):
        dk = jnp.zeros((key_rows_.size, HD), jnp.float32)
        dv = jnp.zeros((key_rows_.size, HD), jnp.float32)
        for half, _, rows, cols in todo:
            probs_b, dscores = grad_terms(
                weight_s[back - 1, key_rows_, cols],
                dprob_s[back - 1, key_rows_, cols],
                peak_s[back - 1, :, cols],
                stat_ref,
                cols,
            )
            dv = dv + dot(probs_b, qo_ref[g, 1, half, rows, :], NN)
            dk = dk + dot(dscores, qo_ref[g, 0, half, rows, :], NN)
            ds_out[back - 1, key_rows_, cols] = dscores
        dkv_s[back - 1, key_rows_, K_COLS] = (dk * INV_ROOT).astype(jnp.bfloat16)
        dkv_s[back - 1, key_rows_, V_COLS] = dv.astype(jnp.bfloat16)

    each(1, both_end, lambda back: grad_block(back, whole, both))
    each(later_count, count, lambda back: grad_block(back, whole, one))

    @pl.when(trim)
    def _():
        grad_block(count - 1, late_rows, both)
        ds_out[count - 2, early_rows, :] = jnp.zeros((tok, 2 * half_cols), jnp.bfloat16)

    part_outs[pairs - 1][...] = dkv_s[pairs - 1]
    for k in range(1, pairs):
        part_outs[k - 1][...] = dkv_s[distance(pair, k, pairs) - 1]


def rest_kernel(
    g, pairs, info_ref, doc_ref, qo_ref, kept_ref, first_stat, stat_ref, ds_ref, kv_ref, *refs
):
    own_out, dq_mine, dq_theirs, dq_s = refs[-4:]
    keys = kv_ref.shape[1]
    tok = keys // 2
    core, chip, _, _, lows = place(info_ref, doc_ref, tok, pairs)
    count, later_count = (blocks_back(chip, low, keys) for low in lows)
    k_tile = kv_ref[0, :, K_COLS]
    dk = jnp.zeros((keys, HD), jnp.float32)
    dv = jnp.zeros((keys, HD), jnp.float32)
    for half, rows, cols in pieces(tok):
        probs_b, dscores = grad_terms(
            kept_ref[g, 0, :, cols], kept_ref[g, 1, :, cols], first_stat[g, 0:1, cols], stat_ref, cols
        )
        dv = dv + dot(probs_b, qo_ref[g, 1, half, rows, :], NN)
        dk = dk + dot(dscores, qo_ref[g, 0, half, rows, :], NN)
        dq_s[:, cols] = dot(k_tile, dscores, TN)
    own_out[:, K_COLS] = dk * INV_ROOT
    own_out[:, V_COLS] = dv

    def query_step(back, carry):
        k_tile = kv_ref[back, :, K_COLS]
        for half, rows, cols in pieces(tok):
            dq_s[:, cols] += dot(k_tile, ds_ref[back - 1, :, cols], TN)
        return carry

    def one_side_step(back, carry):
        k_tile = kv_ref[back, :, K_COLS]
        for at in range(0, PER_KV * tok, keys):
            cols = pl.ds(pl.multiple_of(core * PER_KV * tok + at, keys), keys)
            dq_s[:, cols] += dot(k_tile, ds_ref[back - 1, :, cols], TN)
        return carry

    lax.fori_loop(1, later_count, query_step, 0)
    lax.fori_loop(later_count, count, one_side_step, 0)
    for half, dq_ref in enumerate((dq_mine, dq_theirs)):
        for h in range(PER_KV):
            block = dq_s[:, pl.ds((half * PER_KV + h) * tok, tok)] * INV_ROOT
            dq_ref[:, pl.ds(h * HD, HD)] = block.T.astype(jnp.bfloat16)


def finish_kernel(tok, info_ref, *refs):
    own = refs[:GROUPS]
    back = refs[GROUPS : 2 * GROUPS]
    own_other = refs[2 * GROUPS]
    back_other = refs[2 * GROUPS + 1 : 3 * GROUPS + 1]
    grad_k, grad_v = refs[3 * GROUPS + 1 :]
    core = lax.rem(info_ref[1], 2)
    for g in range(GROUPS):
        mine = own[g][:tok] + back[g][:tok].astype(jnp.float32)
        other = own_other[g] + back_other[g][tok:].astype(jnp.float32)
        for total, side in ((mine, core), (other, 1 - core)):
            cols = pl.ds(pl.multiple_of((side * GROUPS + g) * HD, HD), HD)
            grad_k[:, cols] = total[:, :HD].astype(jnp.bfloat16)
            grad_v[:, cols] = total[:, HD:].astype(jnp.bfloat16)


def nbytes(shapes):
    total = 0
    for s in shapes:
        size = jnp.dtype(s.dtype).itemsize
        for n in s.shape:
            size *= n
        total += size
    return total


def call(kernel, name, scalars, arrays, out_shape, scratch=(), flops=0, passing=(), hbm=(), sems=None):
    smem = pl.BlockSpec(memory_space=pltpu.SMEM)
    vmem = pl.BlockSpec(memory_space=pltpu.VMEM)
    used = nbytes(arrays) + nbytes(out_shape) + nbytes(scratch)
    return pl.pallas_call(
        kernel,
        out_shape=out_shape,
        in_specs=[smem] * len(scalars)
        + [vmem] * len(arrays)
        + [pl.BlockSpec(memory_space=pl.ANY)] * (len(hbm) + len(passing)),
        out_specs=[vmem] * len(out_shape),
        scratch_shapes=[pltpu.VMEM(s.shape, s.dtype) for s in scratch]
        + ([pltpu.SemaphoreType.DMA(sems)] if sems else []),
        compiler_params=pltpu.CompilerParams(vmem_limit_bytes=used + 3 * MIB),
        cost_estimate=pl.CostEstimate(
            flops=flops, bytes_accessed=nbytes(arrays) + nbytes(out_shape), transcendentals=0
        ),
        name=name,
    )(*scalars, *arrays, *hbm, *passing)


def local(queries, keys, values, grad_out, doc_lengths):
    tok = queries.shape[0]
    dp_count = lax.axis_size("dp")
    seq_count = lax.axis_size("seq")
    pairs = seq_count // 2
    dp_idx = lax.axis_index("dp")
    seq_idx = lax.axis_index("seq")
    core = lax.rem(seq_idx, 2)
    pair = seq_idx // 2
    rows = 2 * tok
    lanes = 2 * PER_KV * tok
    f32, bf16 = jnp.float32, jnp.bfloat16
    shape = jax.ShapeDtypeStruct

    def swap(value, k):
        return lax.ppermute(value, "seq", [(i, i ^ k) for i in range(seq_count)])

    k_theirs = swap(keys, 1)
    v_theirs = swap(values, 1)

    def block(g):
        at = (core * GROUPS + g) * HD
        cut = [
            [lax.dynamic_slice_in_dim(t, at, HD, 1) for t in side]
            for side in ((keys, values), (k_theirs, v_theirs))
        ]
        return jnp.concatenate([jnp.concatenate(side, 1) for side in cut], 0)

    own = [block(g) for g in range(GROUPS)]
    prev = [lax.ppermute(o, "dp", [(i, (i + 1) % dp_count) for i in range(dp_count)]) for o in own]
    q_sent, o_sent, _ = lax.optimization_barrier((queries, grad_out, own[-1]))
    q_theirs, o_theirs = swap(q_sent, 1), swap(o_sent, 1)
    info = jnp.stack([dp_idx, seq_idx]).astype(jnp.int32)
    scalars = [info, doc_lengths]

    blocks = []
    for g in range(GROUPS):
        own_now, prev_now = own[g], prev[g]
        if g:
            own_now, *_ = lax.optimization_barrier((own_now, *chosen))
        chosen = [jnp.where((pair ^ k) > pair, own_now, prev_now) for k in range(1, pairs)]
        sent = [swap(c, 2 * k) for k, c in enumerate(chosen, 1)]
        blocks.append([own[g]] + sent + [prev[g]])

    stat = shape((3, lanes), f32)
    unit = 2 * rows * lanes * HD
    outs = call(
        functools.partial(own_kernel, pairs),
        "own",
        scalars,
        own,
        [
            shape((GROUPS, 2, 2, PER_KV * tok, HD), bf16),
            shape((GROUPS, 2, rows, lanes), f32),
            shape((GROUPS, 3, lanes), f32),
        ],
        flops=2 * GROUPS * unit,
        hbm=[queries, grad_out, q_theirs, o_theirs],
        scratch=[shape((GROUPS, 2, 2, tok, PER_KV * HD), bf16)],
        sems=(GROUPS, 2, 2),
    )
    qo, kept, first_stats = outs

    part = shape((rows, 2 * HD), bf16)
    reached, own_parts = [], []
    for g in range(GROUPS):
        stats = first_stats
        if g:
            stats, _ = lax.optimization_barrier((stats, reached[-1][pairs + 2]))
        reached.append(
            call(
                functools.partial(reach_kernel, g, pairs),
                "reach_%d" % g,
                scalars,
                [qo, stats] + blocks[g],
                [part] * pairs
                + [shape((pairs, rows, lanes), bf16), shape((pairs + 1, rows, 2 * HD), bf16), stat],
                [
                    shape((pairs, rows, lanes), f32),
                    shape((pairs, rows, lanes), f32),
                    shape((pairs, 1, lanes), f32),
                    shape((pairs, rows, 2 * HD), bf16),
                ],
                flops=4 * pairs * unit,
                passing=[kept] + [r[pairs] for r in reached],
            )
        )
    own_sums, backs, marks = [], [], []
    for g in range(GROUPS):
        prev_sum = reached[g][pairs - 1].astype(f32)
        own_sum = 0.0
        received = [swap(reached[g][k - 1], 2 * k) for k in range(1, pairs)]
        for k in range(1, pairs):
            back = received[k - 1].astype(f32)
            later = (pair ^ k) > pair
            own_sum = own_sum + jnp.where(later, back, 0.0)
            prev_sum = prev_sum + jnp.where(later, 0.0, back)
        own_sums.append(own_sum)
        prev_sum = prev_sum.astype(bf16)
        marks.append(prev_sum)
        backs.append(
            lax.ppermute(
                prev_sum, "dp", [((i + 1) % dp_count, i) for i in range(dp_count)]
            )
        )
    dq_mine, dq_other = [], []
    for g in range(GROUPS):
        ds, kv, stats = reached[g][pairs:]
        stats, _ = lax.optimization_barrier((stats, marks[g]))
        dq_shape = shape((tok, PER_KV * HD), bf16)
        own_part, mine, theirs = call(
            functools.partial(rest_kernel, g, pairs),
            "rest_%d" % g,
            scalars,
            [qo, kept, first_stats, stats, ds, kv],
            [shape((rows, 2 * HD), f32), dq_shape, dq_shape],
            [shape((HD, lanes), f32)],
            flops=(3 + pairs) * unit,
            passing=[r[pairs] for r in reached[g + 1 :]],
        )
        own_sums[g] = own_sums[g] + own_part
        dq_mine.append(mine)
        dq_other.append(swap(theirs, 1))
    own_other = swap(jnp.stack([t[tok:] for t in own_sums]), 1)
    low = [jnp.where(core == 0, x, y) for x, y in zip(dq_mine, dq_other)]
    high = [jnp.where(core == 0, y, x) for x, y in zip(dq_mine, dq_other)]
    grad_q = jnp.concatenate(low + high, 1)
    grad_q, own_other, backs[-1] = lax.optimization_barrier((grad_q, own_other, backs[-1]))
    back_other = [swap(b, 1) for b in backs]
    out = shape((tok, KVH * HD), bf16)
    grad_k, grad_v = call(
        functools.partial(finish_kernel, tok),
        "finish",
        [info],
        own_sums + backs + [own_other] + back_other,
        [out, out],
    )
    return (grad_q, grad_k, grad_v)


def solution(mesh):
    spec = P(("dp", "seq"), None)
    return jax.shard_map(
        local,
        mesh=mesh,
        in_specs=(spec, spec, spec, spec, P()),
        out_specs=(spec, spec, spec),
        check_vma=False,
    )
```
